512 devices in a mesh: row: 16 (over y, core), col: 32 (over z, x).
Axes of the slice: x: 4, y: 8, z: 8, core: 2. Of those that a mesh axis runs over, the one named last changes fastest.
Arguments:
- fronts: bfloat16 [32, 4096, 4096], P('col', 'row')
- pivots: int32 [32], replicated, may hold values from 1 to 3, as said below
- targets: int32 [32, 16], replicated, may hold values from 0 to 31, as said below
- ancestor: bfloat16 [2, 4096, 8192], P(None, 'row', 'col'), may hold values from -1.5 to 1.5
Outputs:
- factor: float32 [32, 4096, 768], P('col', 'row')
- assembled: float32 [2, 4096, 8192], P(None, 'row', 'col')
The draws below stay inside these ranges and needn't reach their ends.
Inputs may be any that keep to these rules, and one draw needn't show every extreme that they name: `pivots`: every sibling eliminates at least one pivot block column; counts of 1 and of 3 both occur. targets[s, j] is j or j + 16; both ends of the range occur.
All inputs are finite; a program needn't handle non-finite values.
Results may differ from the reference program's by a relative error of at most 0.0011.
Values may be sent and summed in bfloat16 or wider, within the bound.
No kernel may reach another device: no remote copies, remote signals or barrier semaphores. Data moves between devices by JAX's collectives and lax.ppermute only.
A program may use at most 128 MiB of HBM per device.

```python
import jax
import jax.numpy as jnp
from jax import lax

BLOCK = 256
STEPS = 3
FRONT_BLOCKS = 16
FRONT = 4096
ANCESTOR = 8192
SIBLINGS = 32


def draw_fronts(key, part):
    key = jax.random.fold_in(key, 11)
    width = BLOCK * FRONT_BLOCKS
    inner = width // 4

    def single(sibling):
        sub_key = jax.random.fold_in(key, sibling)
        factor_key, diag_key = jax.random.split(sub_key, 2)
        factor_draw = jax.random.normal(factor_key, (width, inner), jnp.float32)
        gram = jnp.dot(factor_draw, factor_draw.T, precision=lax.Precision.HIGHEST) / inner
        gram = 0.5 * (gram + gram.T)
        diagonal = jax.random.uniform(diag_key, (width,), jnp.float32, 0.25, 0.75)
        identity = jnp.arange(width)[:, None] == jnp.arange(width)[None, :]
        matrix = gram + jnp.where(identity, diagonal[:, None], 0.0)
        return matrix
    return lax.map(single, jnp.arange(SIBLINGS, dtype=jnp.int32)).astype(jnp.bfloat16)


def draw_pivots(key, part):
    key = jax.random.fold_in(key, 12)
    value_key, place_key, other_key = jax.random.split(key, 3)
    values = jax.random.randint(value_key, (SIBLINGS,), 1, STEPS + 1)
    place = jax.random.randint(place_key, (), 0, SIBLINGS)
    other = (place + 1 + jax.random.randint(other_key, (), 0, SIBLINGS - 1)) % SIBLINGS
    sibling_ids = jnp.arange(SIBLINGS, dtype=jnp.int32)
    values = jnp.where(sibling_ids == place, STEPS, jnp.where(sibling_ids == other, 1, values))
    return values.astype(jnp.int32)


def draw_targets(key, part):
    key = jax.random.fold_in(key, 13)
    bit_key, high_key, zero_key = jax.random.split(key, 3)
    halves = jax.random.randint(bit_key, (SIBLINGS, FRONT_BLOCKS), 0, 2)
    high_row = jax.random.randint(high_key, (), 0, SIBLINGS)
    zero_row = jax.random.randint(zero_key, (), 0, SIBLINGS)
    sibling_ids = jnp.arange(SIBLINGS, dtype=jnp.int32)[:, None]
    block_ids = jnp.arange(FRONT_BLOCKS, dtype=jnp.int32)[None, :]
    halves = jnp.where((sibling_ids == high_row) & (block_ids == FRONT_BLOCKS - 1), 1, halves)
    halves = jnp.where((sibling_ids == zero_row) & (block_ids == 0), 0, halves)
    return (block_ids + FRONT_BLOCKS * halves).astype(jnp.int32)


def block_scale(rng, dims, cuts, low, top_value):
    def one(dim, blocks):
        heights = jax.random.uniform(jax.random.fold_in(jax.random.fold_in(rng, 6), dim), (blocks,), jnp.float32, low / len(cuts), top_value / len(cuts))
        return jnp.repeat(jnp.exp(heights), dims[dim] // blocks).reshape((-1,) + (1,) * (len(dims) - dim - 1))

    gain = one(*cuts[0])
    for cut in cuts[1:]:
        gain = gain * one(*cut)
    return gain


def centred(stream_key, dims, spread, limit, cuts=(), kind=jnp.bfloat16):
    factor_of = block_scale(stream_key, dims, cuts, -0.22, 0.18) if cuts else 1.0
    array = jax.random.normal(stream_key, dims, jnp.float32) * spread * factor_of
    return jnp.minimum(jnp.maximum(array, -limit), limit).astype(kind)


def setup_inputs(seed: int = 0) -> dict:
    key_of = jax.random.split(jax.random.key(seed), 5)
    return {
        "fronts": draw_fronts(jax.random.fold_in(key_of[4], 71), 0),
        "pivots": draw_pivots(jax.random.fold_in(key_of[4], 71), 0),
        "targets": draw_targets(jax.random.fold_in(key_of[4], 71), 0),
        "ancestor": centred(key_of[3], (2, FRONT, ANCESTOR), 0.1, 1.5, ((1, 16), (2, 32))),
    }


def reference(fronts, pivots, targets, ancestor):
    width = BLOCK * FRONT_BLOCKS
    block_row = (jnp.arange(width, dtype=jnp.int32) // BLOCK).astype(jnp.int32)
    within = (jnp.arange(width, dtype=jnp.int32) % BLOCK).astype(jnp.int32)
    initial = ancestor.astype(jnp.float32).reshape(2 * width, 2 * width)

    def sibling_step(carried, inputs):
        front, pivot_count, target_row = inputs
        working = front.astype(jnp.float32)
        columns = []
        for section in range(STEPS):
            lower_edge = section * BLOCK
            upper_edge = lower_edge + BLOCK
            lower_block = jnp.linalg.cholesky(working[lower_edge:upper_edge, lower_edge:upper_edge])
            solved = jax.scipy.linalg.solve_triangular(lower_block, working[:, lower_edge:upper_edge].T, lower=True).T
            is_active = section < pivot_count
            own_block = jnp.where(block_row[:, None] > section, solved, jnp.zeros_like(solved))
            own_block = own_block.at[lower_edge:upper_edge].set(lower_block)
            columns.append(jnp.where(is_active, own_block, jnp.zeros_like(own_block)))
            outgoing = jnp.where(is_active & (block_row[:, None] > section), solved, jnp.zeros_like(solved)).astype(jnp.bfloat16)
            working = working - jnp.dot(outgoing.astype(jnp.float32), outgoing.T.astype(jnp.float32), preferred_element_type=jnp.float32)
        keep = block_row >= pivot_count
        contribution = jnp.where(keep[:, None] & keep[None, :], working, jnp.zeros_like(working))
        placed = (target_row[block_row] * BLOCK + within).astype(jnp.int32)
        carried = carried.at[placed[:, None], placed[None, :]].add(contribution)
        return (carried, jnp.concatenate(columns, axis=1))
    assembled, factor = lax.scan(sibling_step, initial, (fronts, pivots, targets))
    return (factor, assembled.reshape(2, width, 2 * width))
```

```python
import jax
import jax.numpy as jnp
from jax import lax
from jax.experimental import pallas as pl
from jax.experimental.pallas import tpu as pltpu
from jax.sharding import PartitionSpec as P

STEPS = 3
B = 256
SUB = 8
F32 = jnp.float32
BF16 = jnp.bfloat16
HIGHEST = lax.Precision.HIGHEST


def dot_nt(a, b, precision=None):
    return lax.dot_general(
        a, b, (((1,), (1,)), ((), ())), precision=precision, preferred_element_type=F32
    )


def small_inverse_columns(x, k0):
    sub = lax.broadcasted_iota(jnp.int32, (SUB, 128), 0)
    e = [[None] * SUB for _ in range(SUB)]
    for a in range(SUB):
        for b in range(a + 1):
            e[a][b] = jnp.broadcast_to(x[a : a + 1, k0 + b : k0 + b + 1], (SUB, 128))
    m = [[None] * SUB for _ in range(SUB)]
    for k in range(SUB):
        rc = 1.0 / e[k][k]
        for a in range(k + 1, SUB):
            m[a][k] = e[a][k] * rc
        for a in range(k + 1, SUB):
            for b in range(k + 1, a + 1):
                e[a][b] = e[a][b] - m[a][k] * e[b][k]
    inv = [[None] * SUB for _ in range(SUB)]
    for b in range(SUB):
        for a in range(b + 1, SUB):
            v = m[a][b]
            for c in range(b + 1, a):
                v = v + m[a][c] * inv[c][b]
            inv[a][b] = -v
    piv = e[0][0]
    for a in range(1, SUB):
        piv = jnp.where(sub == a, e[a][a], piv)
    scale = lax.rsqrt(piv)
    cols = []
    for b in range(SUB):
        v = jnp.where(sub == b, 1.0, 0.0)
        for a in range(b + 1, SUB):
            v = jnp.where(sub == a, inv[a][b], v)
        cols.append(v * scale)
    return cols


def cholesky_in_place(t_ref):
    lane = lax.broadcasted_iota(jnp.int32, (SUB, B), 1)
    sub = lax.broadcasted_iota(jnp.int32, (SUB, B), 0)
    for p in range(B // SUB):
        k0 = SUB * p
        x = t_ref[k0 : k0 + SUB, :]
        cols = small_inverse_columns(x, k0)
        r = None
        z = 0.0
        for b in range(SUB):
            wide = jnp.concatenate([cols[b], cols[b]], axis=1)
            term = wide * jnp.broadcast_to(x[b : b + 1, :], (SUB, B))
            r = term if r is None else r + term
            z = jnp.where(lane == k0 + b, wide, z)
        in_block = (lane >= k0) & (lane < k0 + SUB)
        t_ref[k0 : k0 + SUB, :] = jnp.where(in_block & (lane <= k0 + sub), z, r)
        if k0 + SUB < B:
            left = r.T[k0 + SUB :, :]
            update = jnp.dot(
                left, jnp.where(in_block, z, r), precision=HIGHEST, preferred_element_type=F32
            )
            lanes = lax.broadcasted_iota(jnp.int32, (B - k0 - SUB, B), 1)
            old = t_ref[k0 + SUB :, :]
            old = jnp.where((lanes >= k0) & (lanes < k0 + SUB), 0.0, old)
            t_ref[k0 + SUB :, :] = old - update


def chain_kernel(a_ref, low_ref, inv_ref, pan_ref, w_ref, t_ref):
    t = pl.program_id(0)

    @pl.when(t == 0)
    def _():
        w_ref[...] = a_ref[...].astype(F32)

    for s in range(STEPS):

        @pl.when(t == s)
        def _(s=s):
            d = w_ref[s * B : (s + 1) * B, s * B : (s + 1) * B]
            t_ref[...] = 0.5 * (d + d.T)

    cholesky_in_place(t_ref)
    t_val = t_ref[...]
    ri = lax.broadcasted_iota(jnp.int32, (B, B), 0)
    ci = lax.broadcasted_iota(jnp.int32, (B, B), 1)
    inv = jnp.where(ci <= ri, t_val, 0.0)
    inv_ref[0] = inv
    low_ref[0] = jnp.where(ci > ri, t_val, jnp.where(ci == ri, 1.0 / t_val, 0.0)).T

    for s in range(STEPS - 1):

        @pl.when(t == s)
        def _(s=s):
            panels = []
            for r in range(s + 1, STEPS):
                w = w_ref[r * B : (r + 1) * B, s * B : (s + 1) * B]
                panel = dot_nt(w, inv, HIGHEST).astype(BF16)
                panels.append(panel)
                pan_ref[s + r - 1] = panel
            for r in range(s + 1, STEPS):
                for c in range(s + 1, r + 1):
                    w_ref[r * B : (r + 1) * B, c * B : (c + 1) * B] -= dot_nt(
                        panels[r - s - 1], panels[c - s - 1]
                    )


def factor_corner(corner):
    return pl.pallas_call(
        chain_kernel,
        grid=(STEPS,),
        in_specs=[pl.BlockSpec((STEPS * B, STEPS * B), lambda t: (0, 0))],
        out_specs=[
            pl.BlockSpec((1, B, B), lambda t: (t, 0, 0)),
            pl.BlockSpec((1, B, B), lambda t: (t, 0, 0)),
            pl.BlockSpec((STEPS, B, B), lambda t: (0, 0, 0)),
        ],
        out_shape=[
            jax.ShapeDtypeStruct((STEPS, B, B), F32),
            jax.ShapeDtypeStruct((STEPS, B, B), F32),
            jax.ShapeDtypeStruct((STEPS, B, B), BF16),
        ],
        scratch_shapes=[pltpu.VMEM((STEPS * B, STEPS * B), F32), pltpu.VMEM((B, B), F32)],
        compiler_params=pltpu.CompilerParams(vmem_limit_bytes=40 << 20),
        cost_estimate=pl.CostEstimate(
            flops=60_000_000_000, bytes_accessed=4 << 20, transcendentals=0
        ),
    )(corner)


def solve_rows(a, inv_ref, pan_ref, precision):
    solved = []
    panels = []
    for t in range(STEPS):
        w = a[:, t * B : (t + 1) * B].astype(F32)
        for s in range(t):
            w = w - dot_nt(panels[s], pan_ref[t + s - 1])
        x = dot_nt(w, inv_ref[t], precision)
        solved.append(x)
        panels.append(x.astype(BF16))
    return solved, panels


def update_kernel(
    scalars, own_ref, all_ref, low_ref, inv_ref, pan_ref, factor_ref, u_ref, mine_ref
):
    pivots = scalars[0]
    row = scalars[1]

    @pl.when(pl.program_id(0) == 0)
    def _():
        solved, panels = solve_rows(own_ref[...], inv_ref, pan_ref, HIGHEST)
        for t in range(STEPS):
            active = t < pivots
            block = jnp.where(row > t, solved[t], jnp.where(row == t, low_ref[t], 0.0))
            factor_ref[:, t * B : (t + 1) * B] = jnp.where(active, block, 0.0)
            mine_ref[:, t * B : (t + 1) * B] = jnp.where(active, panels[t], 0.0).astype(BF16)

    _, panels = solve_rows(all_ref[0], inv_ref, pan_ref, HIGHEST)
    other = jnp.concatenate(
        [jnp.where(t < pivots, panels[t], 0.0).astype(BF16) for t in range(STEPS)], axis=1
    )
    u_ref[0] = dot_nt(mine_ref[...], other).astype(BF16)


def solve_and_update(scalars, own, gathered, low, inv, pan):
    blocks = gathered.shape[0]
    whole = lambda j: (0, 0, 0)
    return pl.pallas_call(
        update_kernel,
        grid=(blocks,),
        in_specs=[
            pl.BlockSpec(memory_space=pltpu.SMEM),
            pl.BlockSpec((B, STEPS * B), lambda j: (0, 0)),
            pl.BlockSpec((1, B, STEPS * B), lambda j: (j, 0, 0)),
            pl.BlockSpec((STEPS, B, B), whole),
            pl.BlockSpec((STEPS, B, B), whole),
            pl.BlockSpec((STEPS, B, B), whole),
        ],
        out_specs=[
            pl.BlockSpec((B, STEPS * B), lambda j: (0, 0)),
            pl.BlockSpec((1, B, B), lambda j: (j, 0, 0)),
        ],
        out_shape=[
            jax.ShapeDtypeStruct((B, STEPS * B), F32),
            jax.ShapeDtypeStruct((blocks, B, B), BF16),
        ],
        scratch_shapes=[pltpu.VMEM((B, STEPS * B), BF16)],
        compiler_params=pltpu.CompilerParams(vmem_limit_bytes=40 << 20),
        cost_estimate=pl.CostEstimate(
            flops=16_000_000_000, bytes_accessed=16 << 20, transcendentals=0
        ),
    )(scalars, own, gathered, low, inv, pan)


def sum_kernel(slots, f_ref, u_ref, anc_ref, acc_ref):
    k = pl.program_id(0)

    @pl.when(k == 0)
    def _():
        acc_ref[0:2] = anc_ref[...].astype(F32)
        acc_ref[2:4] = jnp.zeros((2, B, B), F32)

    slot = slots[k]

    @pl.when(slot < 4)
    def _():
        acc_ref[slot] += f_ref[0].astype(F32) - u_ref[0].astype(F32)


def sum_blocks(slots, f, u, ancestor):
    count = f.shape[0]
    return pl.pallas_call(
        sum_kernel,
        grid=(count,),
        in_specs=[
            pl.BlockSpec(memory_space=pltpu.SMEM),
            pl.BlockSpec((1, B, B), lambda k: (k, 0, 0)),
            pl.BlockSpec((1, B, B), lambda k: (k, 0, 0)),
            pl.BlockSpec((2, B, B), lambda k: (0, 0, 0)),
        ],
        out_specs=pl.BlockSpec((4, B, B), lambda k: (0, 0, 0)),
        out_shape=jax.ShapeDtypeStruct((4, B, B), F32),
        compiler_params=pltpu.CompilerParams(vmem_limit_bytes=40 << 20),
        cost_estimate=pl.CostEstimate(
            flops=4_000_000, bytes_accessed=6 << 20, transcendentals=0
        ),
    )(slots, f, u, ancestor)


def shards(fronts, pivots, targets, ancestor):
    row = lax.axis_index("row")
    col = lax.axis_index("col")
    cols = lax.axis_size("col")
    blocks = fronts.shape[2] // B
    half = cols // 2
    groups = [list(range(half)), list(range(half, cols))]
    front = fronts[0]

    own = front[:, : STEPS * B]
    gathered = lax.all_gather(own, "row", axis=0, tiled=False)
    f = front.reshape(B, blocks, B).swapaxes(0, 1)
    f = lax.all_to_all(f, "col", 0, 0, axis_index_groups=groups, tiled=True)

    low, inv, pan = factor_corner(gathered[:STEPS].reshape(STEPS * B, STEPS * B))
    scalars = jnp.stack([pivots[col], row.astype(jnp.int32)])
    factor, u = solve_and_update(scalars, own, gathered, low, inv, pan)
    u = lax.all_to_all(u, "col", 0, 0, axis_index_groups=groups, tiled=True)

    side = col // half
    block_col = col % half
    first = side * half
    piv = lax.dynamic_slice_in_dim(pivots, first, half)
    tgt = lax.dynamic_slice_in_dim(targets, first, half, axis=0)
    col_half = lax.dynamic_index_in_dim(tgt, block_col, 1, keepdims=False) // blocks
    row_half = lax.dynamic_index_in_dim(tgt, row, 1, keepdims=False) // blocks
    keep = (block_col >= piv) & (row >= piv)
    slots = jnp.where(keep, jnp.where(col_half == side, 0, 2) + row_half, 4).astype(jnp.int32)
    acc = sum_blocks(slots, f, u, ancestor)
    received = lax.ppermute(acc[2:4], "col", [(c, (c + half) % cols) for c in range(cols)])
    return factor[None], acc[0:2] + received


def solution(mesh):
    in_specs = (P("col", "row", None), P(), P(), P(None, "row", "col"))
    out_specs = (P("col", "row", None), P(None, "row", "col"))
    return jax.shard_map(shards, mesh=mesh, in_specs=in_specs, out_specs=out_specs, check_vma=False)
```

```python
import jax
import jax.numpy as jnp
from jax import lax
from jax.experimental import pallas as pl
from jax.experimental.pallas import tpu as pltpu
from jax.sharding import PartitionSpec as P

STEPS = 3
B = 256
SUB = 8
PANEL = 32
GROUP = 4
VMEM = pl.BlockSpec(memory_space=pltpu.VMEM)
ANY = pl.BlockSpec(memory_space=pl.ANY)
F32 = jnp.float32
BF16 = jnp.bfloat16
HIGHEST = lax.Precision.HIGHEST


def dot_nt(a, b, precision=None):
    return lax.dot_general(
        a, b, (((1,), (1,)), ((), ())), precision=precision, preferred_element_type=F32
    )


def wide(v):
    return jnp.concatenate([v, v], axis=1)


def tree_sum(terms):
    terms = list(terms)
    while len(terms) > 1:
        pairs = [terms[i : i + 2] for i in range(0, len(terms), 2)]
        terms = [p[0] + p[1] if len(p) == 2 else p[0] for p in pairs]
    return terms[0]


def small_ldl(e):
    m = [[None] * SUB for _ in range(SUB)]
    rc = [None] * SUB
    for k in range(SUB):
        rc[k] = 1.0 / e[k][k]
        for a in range(k + 1, SUB):
            m[a][k] = e[a][k] * rc[k]
        for a in range(k + 1, SUB):
            for b in range(k + 1, a + 1):
                e[a][b] = e[a][b] - m[a][k] * e[b][k]
    inv = [[None] * SUB for _ in range(SUB)]
    for b in range(SUB):
        for a in range(b + 1, SUB):
            v = m[a][b]
            for c in range(b + 1, a):
                v = v + m[a][c] * inv[c][b]
            inv[a][b] = -v
    return inv, rc, [e[k][k] for k in range(SUB)]


def factor_tiles(tiles, b0):
    count = len(tiles)
    lane = lax.broadcasted_iota(jnp.int32, (SUB, B), 1)
    sub = lax.broadcasted_iota(jnp.int32, (SUB, B), 0)
    narrow = lax.broadcasted_iota(jnp.int32, (SUB, 128), 0)
    tiles = list(tiles)
    keep = []
    update = []
    for i in range(count):
        k0 = b0 + SUB * i
        x = tiles[i]
        e = [[None] * SUB for _ in range(SUB)]
        for a in range(SUB):
            for b in range(a + 1):
                e[a][b] = jnp.broadcast_to(x[a : a + 1, k0 + b : k0 + b + 1], (SUB, 128))
        inv, rc, d = small_ldl(e)
        cols = []
        for b in range(SUB):
            v = jnp.where(narrow == b, 1.0, 0.0)
            for a in range(b + 1, SUB):
                v = jnp.where(narrow == a, inv[a][b], v)
            cols.append(v)
        pivot = d[0]
        for a in range(1, SUB):
            pivot = jnp.where(narrow == a, d[a], pivot)
        scale = wide(lax.rsqrt(pivot))
        r = tree_sum(
            wide(cols[b]) * jnp.broadcast_to(x[b : b + 1, :], (SUB, B)) for b in range(SUB)
        )
        z = 0.0
        for b in range(SUB):
            z = jnp.where(lane == k0 + b, wide(cols[b]), z)
        in_block = (lane >= k0) & (lane < k0 + SUB)
        y = jnp.where(in_block, z, r)
        if i < count - 1:
            rows = []
            for a in range(SUB):
                v = jnp.where(narrow == a, rc[a], 0.0)
                for b in range(a):
                    v = jnp.where(narrow == b, inv[a][b] * rc[a], v)
                rows.append(v)
            g = tree_sum(
                wide(rows[a]) * jnp.broadcast_to(y[a : a + 1, :], (SUB, B)) for a in range(SUB)
            )
            for j in range(i + 1, count):
                t = tiles[j]
                tiles[j] = jnp.where(in_block, 0.0, t) - tree_sum(
                    jnp.broadcast_to(t[:, k0 + b : k0 + b + 1], (SUB, B))
                    * jnp.broadcast_to(g[b : b + 1, :], (SUB, B))
                    for b in range(SUB)
                )
        scaled = y * scale
        keep.append(jnp.where(in_block & (lane > k0 + sub), r * scale, scaled))
        later = (lane >= k0 + SUB) & (lane < b0 + SUB * count)
        update.append(jnp.where(later, 0.0, scaled))
    return keep, update


def cholesky_in_place(t_ref):
    count = PANEL // SUB
    tiles = [t_ref[SUB * i : SUB * (i + 1), :] for i in range(count)]
    for b0 in range(0, B, PANEL):
        b1 = b0 + PANEL
        keep, update = factor_tiles(tiles, b0)
        for i in range(count):
            t_ref[b0 + SUB * i : b0 + SUB * (i + 1), :] = keep[i]
        if b1 == B:
            break
        right = jnp.concatenate(update, axis=0)
        left = right.T

        def below(lo, hi):
            lanes = lax.broadcasted_iota(jnp.int32, (hi - lo, B), 1)
            old = jnp.where((lanes >= b0) & (lanes < b1), 0.0, t_ref[lo:hi, :])
            return old - jnp.dot(
                left[lo:hi], right, precision=HIGHEST, preferred_element_type=F32
            )

        ahead = below(b1, b1 + PANEL)
        tiles = [ahead[SUB * i : SUB * (i + 1), :] for i in range(count)]
        if b1 + PANEL < B:
            t_ref[b1 + PANEL :, :] = below(b1 + PANEL, B)


def factor_block(d, t_ref, low_ref, inv_ref, s):
    t_ref[...] = 0.5 * (d + d.T)
    cholesky_in_place(t_ref)
    t = t_ref[...]
    ri = lax.broadcasted_iota(jnp.int32, (B, B), 0)
    ci = lax.broadcasted_iota(jnp.int32, (B, B), 1)
    inv = jnp.where(ci <= ri, t, 0.0)
    inv_ref[s] = inv
    low_ref[s] = jnp.where(ci > ri, t, jnp.where(ci == ri, 1.0 / t, 0.0)).T
    return inv


def first_kernel(a_ref, low_ref, inv_ref, t_ref):
    factor_block(a_ref[...].astype(F32), t_ref, low_ref, inv_ref, 0)


def factor_first(block):
    return pl.pallas_call(
        first_kernel,
        in_specs=[VMEM],
        out_specs=[VMEM, VMEM],
        out_shape=[jax.ShapeDtypeStruct((1, B, B), F32)] * 2,
        scratch_shapes=[pltpu.VMEM((B, B), F32)],
        compiler_params=pltpu.CompilerParams(vmem_limit_bytes=40 << 20),
        cost_estimate=pl.CostEstimate(
            flops=10_000_000_000, bytes_accessed=1 << 20, transcendentals=0
        ),
    )(block)


def rest_kernel(a_ref, inv0_ref, low_ref, inv_ref, pan_ref, w_ref, t_ref):
    inv = inv0_ref[0]
    w_ref[...] = a_ref[...].astype(F32)
    for s in range(STEPS - 1):
        panels = []
        for r in range(s + 1, STEPS):
            w = w_ref[(r - 1) * B : r * B, s * B : (s + 1) * B]
            panel = dot_nt(w, inv, HIGHEST).astype(BF16)
            panels.append(panel)
            pan_ref[s + r - 1] = panel
        for r in range(s + 1, STEPS):
            for c in range(s + 1, r + 1):
                w_ref[(r - 1) * B : r * B, c * B : (c + 1) * B] -= dot_nt(
                    panels[r - s - 1], panels[c - s - 1]
                )
        d = w_ref[s * B : (s + 1) * B, (s + 1) * B : (s + 2) * B]
        inv = factor_block(d, t_ref, low_ref, inv_ref, s)


def factor_rest(rows, inv0):
    return pl.pallas_call(
        rest_kernel,
        in_specs=[VMEM, VMEM],
        out_specs=[VMEM, VMEM, VMEM],
        out_shape=[
            jax.ShapeDtypeStruct((STEPS - 1, B, B), F32),
            jax.ShapeDtypeStruct((STEPS - 1, B, B), F32),
            jax.ShapeDtypeStruct((STEPS, B, B), BF16),
        ],
        scratch_shapes=[pltpu.VMEM(((STEPS - 1) * B, STEPS * B), F32), pltpu.VMEM((B, B), F32)],
        compiler_params=pltpu.CompilerParams(vmem_limit_bytes=40 << 20),
        cost_estimate=pl.CostEstimate(
            flops=20_000_000_000, bytes_accessed=4 << 20, transcendentals=0
        ),
    )(rows, inv0)


def split(x):
    high = x.astype(BF16)
    return high, (x - high.astype(F32)).astype(BF16)


def solve_own(a, invs, pan_ref):
    solved = []
    panels = []
    for t in range(STEPS):
        w = a[:, t * B : (t + 1) * B].astype(F32)
        for s in range(t):
            w = w - dot_nt(panels[s], pan_ref[t + s - 1])
        x = dot_nt(w, invs[t], HIGHEST)
        solved.append(x)
        panels.append(x.astype(BF16))
    return solved, panels


def solve_panels(a, parts_ref, pan_ref):
    panels = []
    for t in range(STEPS):
        w = a[:, t * B : (t + 1) * B]
        high, low = parts_ref[t, 0], parts_ref[t, 1]
        if t == 0:
            x = dot_nt(w, high) + dot_nt(w, low)
        else:
            w = w.astype(F32)
            for s in range(t):
                w = w - dot_nt(panels[s], pan_ref[t + s - 1])
            wh, wl = split(w)
            x = dot_nt(wh, high) + (dot_nt(wl, high) + dot_nt(wh, low))
        panels.append(x.astype(BF16))
    return panels


def update_kernel(
    scalars,
    own_ref,
    all_ref,
    low0_ref,
    inv0_ref,
    low_ref,
    inv_ref,
    pan_ref,
    factor_ref,
    u_ref,
    mine_ref,
    parts_ref,
    rows_ref,
    out_ref,
    in_sems,
    out_sems,
):
    groups = u_ref.shape[0] // GROUP

    def fetch(i):
        part = pl.ds(i * GROUP, GROUP)
        return pltpu.make_async_copy(all_ref.at[part], rows_ref.at[part], in_sems.at[i])

    def send(i):
        part = pl.ds(i * GROUP, GROUP)
        return pltpu.make_async_copy(out_ref.at[part], u_ref.at[part], out_sems.at[i])

    for i in range(groups):
        fetch(i).start()
    pivots = scalars[0]
    row = scalars[1]
    lows = [low0_ref[0], low_ref[0], low_ref[1]]
    invs = [inv0_ref[0], inv_ref[0], inv_ref[1]]
    solved, panels = solve_own(own_ref[...], invs, pan_ref)
    for t in range(STEPS):
        active = t < pivots
        block = jnp.where(row > t, solved[t], jnp.where(row == t, lows[t], 0.0))
        factor_ref[:, t * B : (t + 1) * B] = jnp.where(active, block, 0.0)
        mine_ref[:, t * B : (t + 1) * B] = jnp.where(active, panels[t], 0.0).astype(BF16)
        parts_ref[t, 0], parts_ref[t, 1] = split(invs[t])

    def group(i, carry):
        fetch(i).wait()
        a = rows_ref[pl.ds(i * GROUP, GROUP)].reshape(GROUP * B, STEPS * B)
        panels = solve_panels(a, parts_ref, pan_ref)
        other = jnp.concatenate(
            [jnp.where(t < pivots, panels[t], 0.0).astype(BF16) for t in range(STEPS)], axis=1
        )
        for k in range(GROUP):
            out_ref[i * GROUP + k] = dot_nt(
                mine_ref[...], other[k * B : (k + 1) * B]
            ).astype(BF16)
        send(i).start()
        return carry

    lax.fori_loop(0, groups, group, 0)
    for i in range(groups):
        send(i).wait()


def solve_and_update(scalars, own, gathered, low0, inv0, low, inv, pan):
    blocks = gathered.shape[0]
    return pl.pallas_call(
        update_kernel,
        in_specs=[pl.BlockSpec(memory_space=pltpu.SMEM), VMEM, ANY] + [VMEM] * 5,
        out_specs=[VMEM, ANY],
        out_shape=[
            jax.ShapeDtypeStruct((B, STEPS * B), F32),
            jax.ShapeDtypeStruct((blocks, B, B), BF16),
        ],
        scratch_shapes=[
            pltpu.VMEM((B, STEPS * B), BF16),
            pltpu.VMEM((STEPS, 2, B, B), BF16),
            pltpu.VMEM((blocks, B, STEPS * B), BF16),
            pltpu.VMEM((blocks, B, B), BF16),
            pltpu.SemaphoreType.DMA((blocks // GROUP,)),
            pltpu.SemaphoreType.DMA((blocks // GROUP,)),
        ],
        compiler_params=pltpu.CompilerParams(vmem_limit_bytes=48 << 20),
        cost_estimate=pl.CostEstimate(
            flops=16_000_000_000, bytes_accessed=10 << 20, transcendentals=0
        ),
    )(scalars, own, gathered, low0, inv0, low, inv, pan)


def relayout_kernel(x_ref, y_ref, sems):
    copies = [
        pltpu.make_async_copy(x_ref.at[:, j * B : (j + 1) * B], y_ref.at[j], sems.at[j])
        for j in range(y_ref.shape[0])
    ]
    for copy in copies:
        copy.start()
    for copy in copies:
        copy.wait()


def block_columns(front):
    blocks = front.shape[1] // B
    return pl.pallas_call(
        relayout_kernel,
        in_specs=[ANY],
        out_specs=ANY,
        out_shape=jax.ShapeDtypeStruct((blocks, B, B), front.dtype),
        scratch_shapes=[pltpu.SemaphoreType.DMA((blocks,))],
        cost_estimate=pl.CostEstimate(flops=0, bytes_accessed=4 << 20, transcendentals=0),
    )(front)


def start_sum_kernel(slots, x_ref, anc_ref, acc_ref):
    k = pl.program_id(0)

    @pl.when(k == 0)
    def _():
        acc_ref[0:2] = anc_ref[...].astype(F32)
        acc_ref[2:4] = jnp.zeros((2, B, B), F32)

    for i in range(GROUP):
        slot = slots[k * GROUP + i]

        @pl.when(slot < 4)
        def _(i=i, slot=slot):
            acc_ref[slot] += x_ref[i].astype(F32)


def end_sum_kernel(slots, x_ref, start_ref, acc_ref):
    k = pl.program_id(0)

    @pl.when(k == 0)
    def _():
        acc_ref[...] = start_ref[...]

    for i in range(GROUP):
        slot = slots[k * GROUP + i]

        @pl.when(slot < 4)
        def _(i=i, slot=slot):
            acc_ref[slot] -= x_ref[i].astype(F32)


def sum_blocks(kernel, slots, x, start):
    return pl.pallas_call(
        kernel,
        grid=(x.shape[0] // GROUP,),
        in_specs=[
            pl.BlockSpec(memory_space=pltpu.SMEM),
            pl.BlockSpec((GROUP, B, B), lambda k: (k, 0, 0)),
            pl.BlockSpec(start.shape, lambda k: (0, 0, 0)),
        ],
        out_specs=pl.BlockSpec((4, B, B), lambda k: (0, 0, 0)),
        out_shape=jax.ShapeDtypeStruct((4, B, B), F32),
        compiler_params=pltpu.CompilerParams(vmem_limit_bytes=40 << 20),
        cost_estimate=pl.CostEstimate(
            flops=4_000_000_000, bytes_accessed=4 << 20, transcendentals=0
        ),
    )(slots, x, start)


def broadcast_first(block, row):
    size = lax.axis_size("row")
    step = size // 2
    while step:
        pairs = [(i, i + step) for i in range(0, size, 2 * step)]
        got = lax.ppermute(block, "row", pairs)
        block = jnp.where(row % (2 * step) == step, got, block)
        step //= 2
    return block


def shards(fronts, pivots, targets, ancestor):
    row = lax.axis_index("row")
    col = lax.axis_index("col")
    cols = lax.axis_size("col")
    blocks = fronts.shape[2] // B
    half = cols // 2
    groups = [list(range(half)), list(range(half, cols))]
    front = fronts[0]

    side = col // half
    block_col = col % half
    first = side * half
    piv = lax.dynamic_slice_in_dim(pivots, first, half)
    tgt = lax.dynamic_slice_in_dim(targets, first, half, axis=0)
    col_half = lax.dynamic_index_in_dim(tgt, block_col, 1, keepdims=False) // blocks
    row_half = lax.dynamic_index_in_dim(tgt, row, 1, keepdims=False) // blocks
    keep = (block_col >= piv) & (row >= piv)
    slots = jnp.where(keep, jnp.where(col_half == side, 0, 2) + row_half, 4).astype(jnp.int32)
    scalars = jnp.stack([pivots[col], row.astype(jnp.int32)])

    own, corner = lax.optimization_barrier((front[:, : STEPS * B], front[:, :B]))
    gathered = lax.all_gather(own, "row", axis=0, tiled=False)
    corner = broadcast_first(corner, row)
    low0, inv0 = factor_first(corner)
    f = lax.all_to_all(
        block_columns(front), "col", 0, 0, axis_index_groups=groups, tiled=True
    )

    low, inv, pan = factor_rest(gathered[1:STEPS].reshape((STEPS - 1) * B, STEPS * B), inv0)
    factor, u = solve_and_update(scalars, own, gathered, low0, inv0, low, inv, pan)
    u = lax.all_to_all(u, "col", 0, 0, axis_index_groups=groups, tiled=True)

    acc = sum_blocks(start_sum_kernel, slots, f, ancestor)
    acc = sum_blocks(end_sum_kernel, slots, u, acc)
    received = lax.ppermute(acc[2:4], "col", [(c, (c + half) % cols) for c in range(cols)])
    return factor[None], acc[0:2] + received


def solution(mesh):
    in_specs = (P("col", "row", None), P(), P(), P(None, "row", "col"))
    out_specs = (P("col", "row", None), P(None, "row", "col"))
    return jax.shard_map(shards, mesh=mesh, in_specs=in_specs, out_specs=out_specs, check_vma=False)
```

```python
import jax
import jax.numpy as jnp
from jax import lax
from jax.experimental import pallas as pl
from jax.experimental.pallas import tpu as pltpu
from jax.sharding import PartitionSpec as P

STEPS = 3
B = 256
SUB = 8
PANEL = 32
GROUP = 4
VMEM = pl.BlockSpec(memory_space=pltpu.VMEM)
ANY = pl.BlockSpec(memory_space=pl.ANY)
F32 = jnp.float32
BF16 = jnp.bfloat16
HIGHEST = lax.Precision.HIGHEST


def dot_nt(a, b, precision=None):
    return lax.dot_general(
        a, b, (((1,), (1,)), ((), ())), precision=precision, preferred_element_type=F32
    )


def wide(v):
    return jnp.concatenate([v, v], axis=1)


def tree_sum(terms):
    terms = list(terms)
    while len(terms) > 1:
        pairs = [terms[i : i + 2] for i in range(0, len(terms), 2)]
        terms = [p[0] + p[1] if len(p) == 2 else p[0] for p in pairs]
    return terms[0]


def small_ldl(e):
    m = [[None] * SUB for _ in range(SUB)]
    rc = [None] * SUB
    for k in range(SUB):
        rc[k] = 1.0 / e[k][k]
        for a in range(k + 1, SUB):
            m[a][k] = e[a][k] * rc[k]
        for a in range(k + 1, SUB):
            for b in range(k + 1, a + 1):
                e[a][b] = e[a][b] - m[a][k] * e[b][k]
    inv = [[None] * SUB for _ in range(SUB)]
    for b in range(SUB):
        for a in range(b + 1, SUB):
            v = m[a][b]
            for c in range(b + 1, a):
                v = v + m[a][c] * inv[c][b]
            inv[a][b] = -v
    return inv, rc, [e[k][k] for k in range(SUB)]


def factor_tiles(tiles, b0):
    count = len(tiles)
    lane = lax.broadcasted_iota(jnp.int32, (SUB, B), 1)
    sub = lax.broadcasted_iota(jnp.int32, (SUB, B), 0)
    narrow = lax.broadcasted_iota(jnp.int32, (SUB, 128), 0)
    tiles = list(tiles)
    keep = []
    update = []
    for i in range(count):
        k0 = b0 + SUB * i
        x = tiles[i]
        e = [[None] * SUB for _ in range(SUB)]
        for a in range(SUB):
            for b in range(a + 1):
                e[a][b] = jnp.broadcast_to(x[a : a + 1, k0 + b : k0 + b + 1], (SUB, 128))
        inv, rc, d = small_ldl(e)
        cols = []
        for b in range(SUB):
            v = jnp.where(narrow == b, 1.0, 0.0)
            for a in range(b + 1, SUB):
                v = jnp.where(narrow == a, inv[a][b], v)
            cols.append(v)
        pivot = d[0]
        for a in range(1, SUB):
            pivot = jnp.where(narrow == a, d[a], pivot)
        scale = wide(lax.rsqrt(pivot))
        r = tree_sum(
            wide(cols[b]) * jnp.broadcast_to(x[b : b + 1, :], (SUB, B)) for b in range(SUB)
        )
        z = 0.0
        for b in range(SUB):
            z = jnp.where(lane == k0 + b, wide(cols[b]), z)
        in_block = (lane >= k0) & (lane < k0 + SUB)
        y = jnp.where(in_block, z, r)
        if i < count - 1:
            rows = []
            for a in range(SUB):
                v = jnp.where(narrow == a, rc[a], 0.0)
                for b in range(a):
                    v = jnp.where(narrow == b, inv[a][b] * rc[a], v)
                rows.append(v)
            g = tree_sum(
                wide(rows[a]) * jnp.broadcast_to(y[a : a + 1, :], (SUB, B)) for a in range(SUB)
            )
            for j in range(i + 1, count):
                t = tiles[j]
                tiles[j] = jnp.where(in_block, 0.0, t) - tree_sum(
                    jnp.broadcast_to(t[:, k0 + b : k0 + b + 1], (SUB, B))
                    * jnp.broadcast_to(g[b : b + 1, :], (SUB, B))
                    for b in range(SUB)
                )
        scaled = y * scale
        keep.append(jnp.where(in_block & (lane > k0 + sub), r * scale, scaled))
        later = (lane >= k0 + SUB) & (lane < b0 + SUB * count)
        update.append(jnp.where(later, 0.0, scaled))
    return keep, update


def cholesky_in_place(t_ref):
    count = PANEL // SUB
    tiles = [t_ref[SUB * i : SUB * (i + 1), :] for i in range(count)]
    for b0 in range(0, B, PANEL):
        b1 = b0 + PANEL
        keep, update = factor_tiles(tiles, b0)
        for i in range(count):
            t_ref[b0 + SUB * i : b0 + SUB * (i + 1), :] = keep[i]
        if b1 == B:
            break
        right = jnp.concatenate(update, axis=0)
        left = right.T

        def below(lo, hi):
            lanes = lax.broadcasted_iota(jnp.int32, (hi - lo, B), 1)
            old = jnp.where((lanes >= b0) & (lanes < b1), 0.0, t_ref[lo:hi, :])
            return old - jnp.dot(
                left[lo:hi], right, precision=HIGHEST, preferred_element_type=F32
            )

        ahead = below(b1, b1 + PANEL)
        tiles = [ahead[SUB * i : SUB * (i + 1), :] for i in range(count)]
        if b1 + PANEL < B:
            t_ref[b1 + PANEL :, :] = below(b1 + PANEL, B)


def factor_block(d, t_ref, low_ref, inv_ref, s):
    t_ref[...] = 0.5 * (d + d.T)
    cholesky_in_place(t_ref)
    t = t_ref[...]
    ri = lax.broadcasted_iota(jnp.int32, (B, B), 0)
    ci = lax.broadcasted_iota(jnp.int32, (B, B), 1)
    inv = jnp.where(ci <= ri, t, 0.0)
    inv_ref[s] = inv
    low_ref[s] = jnp.where(ci > ri, t, jnp.where(ci == ri, 1.0 / t, 0.0)).T
    return inv


def first_kernel(a_ref, low_ref, inv_ref, t_ref):
    factor_block(a_ref[...].astype(F32), t_ref, low_ref, inv_ref, 0)


def factor_first(block):
    return pl.pallas_call(
        first_kernel,
        in_specs=[VMEM],
        out_specs=[VMEM, VMEM],
        out_shape=[jax.ShapeDtypeStruct((1, B, B), F32)] * 2,
        scratch_shapes=[pltpu.VMEM((B, B), F32)],
        compiler_params=pltpu.CompilerParams(vmem_limit_bytes=40 << 20),
        cost_estimate=pl.CostEstimate(
            flops=10_000_000_000, bytes_accessed=1 << 20, transcendentals=0
        ),
    )(block)


def rest_kernel(a_ref, inv0_ref, low_ref, inv_ref, pan_ref, w_ref, t_ref):
    inv = inv0_ref[0]
    w_ref[...] = a_ref[...].astype(F32)
    for s in range(STEPS - 1):
        panels = []
        for r in range(s + 1, STEPS):
            w = w_ref[(r - 1) * B : r * B, s * B : (s + 1) * B]
            panel = dot_nt(w, inv, HIGHEST).astype(BF16)
            panels.append(panel)
            pan_ref[s + r - 1] = panel
        for r in range(s + 1, STEPS):
            for c in range(s + 1, r + 1):
                w_ref[(r - 1) * B : r * B, c * B : (c + 1) * B] -= dot_nt(
                    panels[r - s - 1], panels[c - s - 1]
                )
        d = w_ref[s * B : (s + 1) * B, (s + 1) * B : (s + 2) * B]
        inv = factor_block(d, t_ref, low_ref, inv_ref, s)


def factor_rest(rows, inv0):
    return pl.pallas_call(
        rest_kernel,
        in_specs=[VMEM, VMEM],
        out_specs=[VMEM, VMEM, VMEM],
        out_shape=[
            jax.ShapeDtypeStruct((STEPS - 1, B, B), F32),
            jax.ShapeDtypeStruct((STEPS - 1, B, B), F32),
            jax.ShapeDtypeStruct((STEPS, B, B), BF16),
        ],
        scratch_shapes=[pltpu.VMEM(((STEPS - 1) * B, STEPS * B), F32), pltpu.VMEM((B, B), F32)],
        compiler_params=pltpu.CompilerParams(vmem_limit_bytes=40 << 20),
        cost_estimate=pl.CostEstimate(
            flops=20_000_000_000, bytes_accessed=4 << 20, transcendentals=0
        ),
    )(rows, inv0)


def split(x):
    high = x.astype(BF16)
    return high, (x - high.astype(F32)).astype(BF16)


def solve_own(a, invs, pan_ref):
    solved = []
    panels = []
    for t in range(STEPS):
        w = a[:, t * B : (t + 1) * B].astype(F32)
        for s in range(t):
            w = w - dot_nt(panels[s], pan_ref[t + s - 1])
        x = dot_nt(w, invs[t], HIGHEST)
        solved.append(x)
        panels.append(x.astype(BF16))
    return solved, panels


def solve_panels(a, parts_ref, pan_ref):
    panels = []
    for t in range(STEPS):
        w = a[:, t * B : (t + 1) * B]
        high, low = parts_ref[t, 0], parts_ref[t, 1]
        if t == 0:
            x = dot_nt(w, high) + dot_nt(w, low)
        else:
            w = w.astype(F32)
            for s in range(t):
                w = w - dot_nt(panels[s], pan_ref[t + s - 1])
            wh, wl = split(w)
            x = dot_nt(wh, high) + (dot_nt(wl, high) + dot_nt(wh, low))
        panels.append(x.astype(BF16))
    return panels


def update_kernel(
    scalars,
    own_ref,
    all_ref,
    low0_ref,
    inv0_ref,
    low_ref,
    inv_ref,
    pan_ref,
    factor_ref,
    u_ref,
    mine_ref,
    parts_ref,
    rows_ref,
    out_ref,
    in_sems,
    out_sems,
):
    groups = u_ref.shape[0] // GROUP

    def fetch(i):
        part = pl.ds(i * GROUP, GROUP)
        return pltpu.make_async_copy(all_ref.at[part], rows_ref.at[part], in_sems.at[i])

    def send(i):
        part = pl.ds(i * GROUP, GROUP)
        return pltpu.make_async_copy(out_ref.at[part], u_ref.at[part], out_sems.at[i])

    for i in range(groups):
        fetch(i).start()
    pivots = scalars[0]
    row = scalars[1]
    lows = [low0_ref[0], low_ref[0], low_ref[1]]
    invs = [inv0_ref[0], inv_ref[0], inv_ref[1]]
    solved, panels = solve_own(own_ref[...], invs, pan_ref)
    for t in range(STEPS):
        active = t < pivots
        block = jnp.where(row > t, solved[t], jnp.where(row == t, lows[t], 0.0))
        factor_ref[:, t * B : (t + 1) * B] = jnp.where(active, block, 0.0)
        mine_ref[:, t * B : (t + 1) * B] = jnp.where(active, panels[t], 0.0).astype(BF16)
        parts_ref[t, 0], parts_ref[t, 1] = split(invs[t])

    def group(i, carry):
        fetch(i).wait()
        a = rows_ref[pl.ds(i * GROUP, GROUP)].reshape(GROUP * B, STEPS * B)
        panels = solve_panels(a, parts_ref, pan_ref)
        other = jnp.concatenate(
            [jnp.where(t < pivots, panels[t], 0.0).astype(BF16) for t in range(STEPS)], axis=1
        )
        for k in range(GROUP):
            out_ref[i * GROUP + k] = dot_nt(
                mine_ref[...], other[k * B : (k + 1) * B]
            ).astype(BF16)
        send(i).start()
        return carry

    lax.fori_loop(0, groups, group, 0)
    for i in range(groups):
        send(i).wait()


def solve_and_update(scalars, own, gathered, low0, inv0, low, inv, pan):
    blocks = gathered.shape[0]
    return pl.pallas_call(
        update_kernel,
        in_specs=[pl.BlockSpec(memory_space=pltpu.SMEM), VMEM, ANY] + [VMEM] * 5,
        out_specs=[VMEM, ANY],
        out_shape=[
            jax.ShapeDtypeStruct((B, STEPS * B), F32),
            jax.ShapeDtypeStruct((blocks, B, B), BF16),
        ],
        scratch_shapes=[
            pltpu.VMEM((B, STEPS * B), BF16),
            pltpu.VMEM((STEPS, 2, B, B), BF16),
            pltpu.VMEM((blocks, B, STEPS * B), BF16),
            pltpu.VMEM((blocks, B, B), BF16),
            pltpu.SemaphoreType.DMA((blocks // GROUP,)),
            pltpu.SemaphoreType.DMA((blocks // GROUP,)),
        ],
        compiler_params=pltpu.CompilerParams(vmem_limit_bytes=48 << 20),
        cost_estimate=pl.CostEstimate(
            flops=16_000_000_000, bytes_accessed=10 << 20, transcendentals=0
        ),
    )(scalars, own, gathered, low0, inv0, low, inv, pan)


def relayout_kernel(x_ref, y_ref):
    for i in range(GROUP):
        y_ref[i] = x_ref[:, i * B : (i + 1) * B]


def block_columns(front):
    blocks = front.shape[1] // B
    return pl.pallas_call(
        relayout_kernel,
        grid=(blocks // GROUP,),
        in_specs=[pl.BlockSpec((B, GROUP * B), lambda j: (0, j))],
        out_specs=pl.BlockSpec((GROUP, B, B), lambda j: (j, 0, 0)),
        out_shape=jax.ShapeDtypeStruct((blocks, B, B), front.dtype),
        cost_estimate=pl.CostEstimate(flops=0, bytes_accessed=4 << 20, transcendentals=0),
    )(front)


def start_sum_kernel(slots, x_ref, anc_ref, acc_ref):
    k = pl.program_id(0)

    @pl.when(k == 0)
    def _():
        acc_ref[0:2] = anc_ref[...].astype(F32)
        acc_ref[2:4] = jnp.zeros((2, B, B), F32)

    for i in range(GROUP):
        slot = slots[k * GROUP + i]

        @pl.when(slot < 4)
        def _(i=i, slot=slot):
            acc_ref[slot] += x_ref[i].astype(F32)


def end_sum_kernel(slots, x_ref, start_ref, acc_ref):
    k = pl.program_id(0)

    @pl.when(k == 0)
    def _():
        acc_ref[...] = start_ref[...]

    for i in range(GROUP):
        slot = slots[k * GROUP + i]

        @pl.when(slot < 4)
        def _(i=i, slot=slot):
            acc_ref[slot] -= x_ref[i].astype(F32)


def sum_blocks(kernel, slots, x, start):
    return pl.pallas_call(
        kernel,
        grid=(x.shape[0] // GROUP,),
        in_specs=[
            pl.BlockSpec(memory_space=pltpu.SMEM),
            pl.BlockSpec((GROUP, B, B), lambda k: (k, 0, 0)),
            pl.BlockSpec(start.shape, lambda k: (0, 0, 0)),
        ],
        out_specs=pl.BlockSpec((4, B, B), lambda k: (0, 0, 0)),
        out_shape=jax.ShapeDtypeStruct((4, B, B), F32),
        compiler_params=pltpu.CompilerParams(vmem_limit_bytes=40 << 20),
        cost_estimate=pl.CostEstimate(
            flops=4_000_000_000, bytes_accessed=4 << 20, transcendentals=0
        ),
    )(slots, x, start)


def broadcast_first(block, row):
    size = lax.axis_size("row")
    step = size // 2
    while step:
        pairs = [(i, i + step) for i in range(0, size, 2 * step)]
        got = lax.ppermute(block, "row", pairs)
        block = jnp.where(row % (2 * step) == step, got, block)
        step //= 2
    return block


def shards(fronts, pivots, targets, ancestor):
    row = lax.axis_index("row")
    col = lax.axis_index("col")
    cols = lax.axis_size("col")
    blocks = fronts.shape[2] // B
    half = cols // 2
    groups = [list(range(half)), list(range(half, cols))]
    front = fronts[0]

    side = col // half
    block_col = col % half
    first = side * half
    piv = lax.dynamic_slice_in_dim(pivots, first, half)
    tgt = lax.dynamic_slice_in_dim(targets, first, half, axis=0)
    col_half = lax.dynamic_index_in_dim(tgt, block_col, 1, keepdims=False) // blocks
    row_half = lax.dynamic_index_in_dim(tgt, row, 1, keepdims=False) // blocks
    keep = (block_col >= piv) & (row >= piv)
    slots = jnp.where(keep, jnp.where(col_half == side, 0, 2) + row_half, 4).astype(jnp.int32)
    scalars = jnp.stack([pivots[col], row.astype(jnp.int32)])

    own, corner = lax.optimization_barrier((front[:, : STEPS * B], front[:, :B]))
    gathered = lax.all_gather(own, "row", axis=0, tiled=False)
    corner = broadcast_first(corner, row)
    low0, inv0 = factor_first(corner)
    f = lax.all_to_all(
        block_columns(front), "col", 0, 0, axis_index_groups=groups, tiled=True
    )

    low, inv, pan = factor_rest(gathered[1:STEPS].reshape((STEPS - 1) * B, STEPS * B), inv0)
    factor, u = solve_and_update(scalars, own, gathered, low0, inv0, low, inv, pan)
    u = lax.all_to_all(u, "col", 0, 0, axis_index_groups=groups, tiled=True)

    acc = sum_blocks(start_sum_kernel, slots, f, ancestor)
    acc = sum_blocks(end_sum_kernel, slots, u, acc)
    received = lax.ppermute(acc[2:4], "col", [(c, (c + half) % cols) for c in range(cols)])
    return factor[None], acc[0:2] + received


def solution(mesh):
    in_specs = (P("col", "row", None), P(), P(), P(None, "row", "col"))
    out_specs = (P("col", "row", None), P(None, "row", "col"))
    return jax.shard_map(shards, mesh=mesh, in_specs=in_specs, out_specs=out_specs, check_vma=False)
```

```python
import jax
import jax.numpy as jnp
from jax import lax
from jax.experimental import pallas as pl
from jax.experimental.pallas import tpu as pltpu
from jax.sharding import PartitionSpec as P

STEPS = 3
B = 256
SUB = 8
PANEL = 32
GROUP = 4
H = B // 2
EXTRA = 16
VMEM = pl.BlockSpec(memory_space=pltpu.VMEM)
ANY = pl.BlockSpec(memory_space=pl.ANY)
F32 = jnp.float32
BF16 = jnp.bfloat16
HIGHEST = lax.Precision.HIGHEST


def dot_nt(a, b, precision=None):
    return lax.dot_general(
        a, b, (((1,), (1,)), ((), ())), precision=precision, preferred_element_type=F32
    )


def wide(v):
    return jnp.concatenate([v, v], axis=1)


def tree_sum(terms):
    terms = list(terms)
    while len(terms) > 1:
        pairs = [terms[i : i + 2] for i in range(0, len(terms), 2)]
        terms = [p[0] + p[1] if len(p) == 2 else p[0] for p in pairs]
    return terms[0]


def small_ldl(e):
    m = [[None] * SUB for _ in range(SUB)]
    rc = [None] * SUB
    for k in range(SUB):
        rc[k] = 1.0 / e[k][k]
        for a in range(k + 1, SUB):
            m[a][k] = e[a][k] * rc[k]
        for a in range(k + 1, SUB):
            for b in range(k + 1, a + 1):
                e[a][b] = e[a][b] - m[a][k] * e[b][k]
    inv = [[None] * SUB for _ in range(SUB)]
    for b in range(SUB):
        for a in range(b + 1, SUB):
            v = m[a][b]
            for c in range(b + 1, a):
                v = v + m[a][c] * inv[c][b]
            inv[a][b] = -v
    return inv, rc, [e[k][k] for k in range(SUB)]


def factor_tiles(tiles, b0):
    count = len(tiles)
    lane = lax.broadcasted_iota(jnp.int32, (SUB, B), 1)
    sub = lax.broadcasted_iota(jnp.int32, (SUB, B), 0)
    narrow = lax.broadcasted_iota(jnp.int32, (SUB, 128), 0)
    tiles = list(tiles)
    keep = []
    update = []
    for i in range(count):
        k0 = b0 + SUB * i
        x = tiles[i]
        e = [[None] * SUB for _ in range(SUB)]
        for a in range(SUB):
            for b in range(a + 1):
                e[a][b] = jnp.broadcast_to(x[a : a + 1, k0 + b : k0 + b + 1], (SUB, 128))
        inv, rc, d = small_ldl(e)
        cols = []
        for b in range(SUB):
            v = jnp.where(narrow == b, 1.0, 0.0)
            for a in range(b + 1, SUB):
                v = jnp.where(narrow == a, inv[a][b], v)
            cols.append(v)
        pivot = d[0]
        for a in range(1, SUB):
            pivot = jnp.where(narrow == a, d[a], pivot)
        scale = wide(lax.rsqrt(pivot))
        r = tree_sum(
            wide(cols[b]) * jnp.broadcast_to(x[b : b + 1, :], (SUB, B)) for b in range(SUB)
        )
        z = 0.0
        for b in range(SUB):
            z = jnp.where(lane == k0 + b, wide(cols[b]), z)
        in_block = (lane >= k0) & (lane < k0 + SUB)
        y = jnp.where(in_block, z, r)
        if i < count - 1:
            rows = []
            for a in range(SUB):
                v = jnp.where(narrow == a, rc[a], 0.0)
                for b in range(a):
                    v = jnp.where(narrow == b, inv[a][b] * rc[a], v)
                rows.append(v)
            g = tree_sum(
                wide(rows[a]) * jnp.broadcast_to(y[a : a + 1, :], (SUB, B)) for a in range(SUB)
            )
            for j in range(i + 1, count):
                t = tiles[j]
                tiles[j] = jnp.where(in_block, 0.0, t) - tree_sum(
                    jnp.broadcast_to(t[:, k0 + b : k0 + b + 1], (SUB, B))
                    * jnp.broadcast_to(g[b : b + 1, :], (SUB, B))
                    for b in range(SUB)
                )
        scaled = y * scale
        keep.append(jnp.where(in_block & (lane > k0 + sub), r * scale, scaled))
        later = (lane >= k0 + SUB) & (lane < b0 + SUB * count)
        update.append(jnp.where(later, 0.0, scaled))
    return keep, update


def cholesky_in_place(t_ref):
    count = PANEL // SUB
    tiles = [t_ref[SUB * i : SUB * (i + 1), :] for i in range(count)]
    for b0 in range(0, B, PANEL):
        b1 = b0 + PANEL
        keep, update = factor_tiles(tiles, b0)
        for i in range(count):
            t_ref[b0 + SUB * i : b0 + SUB * (i + 1), :] = keep[i]
        if b1 == B:
            break
        right = jnp.concatenate(update, axis=0)
        left = right.T

        def below(lo, hi):
            lanes = lax.broadcasted_iota(jnp.int32, (hi - lo, B), 1)
            old = jnp.where((lanes >= b0) & (lanes < b1), 0.0, t_ref[lo:hi, :])
            return old - jnp.dot(
                left[lo:hi], right, precision=HIGHEST, preferred_element_type=F32
            )

        ahead = below(b1, b1 + PANEL)
        tiles = [ahead[SUB * i : SUB * (i + 1), :] for i in range(count)]
        if b1 + PANEL < B:
            t_ref[b1 + PANEL :, :] = below(b1 + PANEL, B)


def factor_block(d, t_ref, low_ref, inv_ref, s):
    t_ref[...] = 0.5 * (d + d.T)
    cholesky_in_place(t_ref)
    t = t_ref[...]
    ri = lax.broadcasted_iota(jnp.int32, (B, B), 0)
    ci = lax.broadcasted_iota(jnp.int32, (B, B), 1)
    inv = jnp.where(ci <= ri, t, 0.0)
    inv_ref[s] = inv
    low_ref[s] = jnp.where(ci > ri, t, jnp.where(ci == ri, 1.0 / t, 0.0)).T
    return inv


def first_kernel(a_ref, low_ref, inv_ref, t_ref):
    factor_block(a_ref[...].astype(F32), t_ref, low_ref, inv_ref, 0)


def factor_first(block):
    return pl.pallas_call(
        first_kernel,
        in_specs=[VMEM],
        out_specs=[VMEM, VMEM],
        out_shape=[jax.ShapeDtypeStruct((1, B, B), F32)] * 2,
        scratch_shapes=[pltpu.VMEM((B, B), F32)],
        compiler_params=pltpu.CompilerParams(vmem_limit_bytes=40 << 20),
        cost_estimate=pl.CostEstimate(
            flops=10_000_000_000, bytes_accessed=1 << 20, transcendentals=0
        ),
    )(block)


def rest_kernel(a_ref, inv0_ref, low_ref, inv_ref, pan_ref, w_ref, t_ref):
    inv = inv0_ref[0]
    w_ref[...] = a_ref[...].astype(F32)
    for s in range(STEPS - 1):
        panels = []
        for r in range(s + 1, STEPS):
            w = w_ref[(r - 1) * B : r * B, s * B : (s + 1) * B]
            panel = dot_nt(w, inv, HIGHEST).astype(BF16)
            panels.append(panel)
            pan_ref[s + r - 1] = panel
        for r in range(s + 1, STEPS):
            for c in range(s + 1, r + 1):
                w_ref[(r - 1) * B : r * B, c * B : (c + 1) * B] -= dot_nt(
                    panels[r - s - 1], panels[c - s - 1]
                )
        d = w_ref[s * B : (s + 1) * B, (s + 1) * B : (s + 2) * B]
        inv = factor_block(d, t_ref, low_ref, inv_ref, s)


def factor_rest(rows, inv0):
    return pl.pallas_call(
        rest_kernel,
        in_specs=[VMEM, VMEM],
        out_specs=[VMEM, VMEM, VMEM],
        out_shape=[
            jax.ShapeDtypeStruct((STEPS - 1, B, B), F32),
            jax.ShapeDtypeStruct((STEPS - 1, B, B), F32),
            jax.ShapeDtypeStruct((STEPS, B, B), BF16),
        ],
        scratch_shapes=[pltpu.VMEM(((STEPS - 1) * B, STEPS * B), F32), pltpu.VMEM((B, B), F32)],
        compiler_params=pltpu.CompilerParams(vmem_limit_bytes=40 << 20),
        cost_estimate=pl.CostEstimate(
            flops=20_000_000_000, bytes_accessed=4 << 20, transcendentals=0
        ),
    )(rows, inv0)


def split(x):
    high = x.astype(BF16)
    return high, (x - high.astype(F32)).astype(BF16)


def solve_own(a, invs, pan_ref):
    solved = []
    panels = []
    for t in range(STEPS):
        w = a[:, t * B : (t + 1) * B].astype(F32)
        for s in range(t):
            w = w - dot_nt(panels[s], pan_ref[t + s - 1])
        x = dot_nt(w, invs[t], HIGHEST)
        solved.append(x)
        panels.append(x.astype(BF16))
    return solved, panels


def solve_panels(a, parts_ref, pan_ref):
    panels = []
    for t in range(STEPS):
        w = a[:, t * B : (t + 1) * B]
        high, low = parts_ref[t, 0], parts_ref[t, 1]
        if t == 0:
            x = dot_nt(w, high) + dot_nt(w, low)
        else:
            w = w.astype(F32)
            for s in range(t):
                w = w - dot_nt(panels[s], pan_ref[t + s - 1])
            wh, wl = split(w)
            x = dot_nt(wh, high) + (dot_nt(wl, high) + dot_nt(wh, low))
        panels.append(x.astype(BF16))
    return panels


def half_update(row, j, mine_ref, other, out_ref):
    @pl.when(row < j)
    def _():
        out_ref[j, :H] = dot_nt(mine_ref[:H, :], other).astype(BF16)
        out_ref[j, H:] = jnp.zeros((EXTRA, B), BF16)

    @pl.when(row > j)
    def _():
        out_ref[j, :H] = dot_nt(other[H:], mine_ref[...]).astype(BF16)
        out_ref[j, H:] = jnp.zeros((EXTRA, B), BF16)

    @pl.when(row == j)
    def _():
        top = dot_nt(mine_ref[:H, :], mine_ref[...])
        last = dot_nt(mine_ref[H:, :], mine_ref[H:, :])
        ri = lax.broadcasted_iota(jnp.int32, (H, H), 0)
        ci = lax.broadcasted_iota(jnp.int32, (H, H), 1)
        first = jnp.where(ri >= ci, top[:, :H], last)
        out_ref[j, :H] = jnp.concatenate([first, top[:, H:]], axis=1).astype(BF16)
        diagonal = jnp.sum(jnp.where(ri == ci, last, 0.0), axis=0, keepdims=True)
        diagonal = jnp.concatenate([diagonal, jnp.zeros((1, H), F32)], axis=1)
        out_ref[j, H:] = jnp.broadcast_to(diagonal, (EXTRA, B)).astype(BF16)


def update_kernel(
    scalars,
    own_ref,
    all_ref,
    low0_ref,
    inv0_ref,
    low_ref,
    inv_ref,
    pan_ref,
    factor_ref,
    u_ref,
    mine_ref,
    parts_ref,
    rows_ref,
    out_ref,
    in_sems,
    out_sems,
):
    groups = u_ref.shape[0] // GROUP

    def fetch(i):
        part = pl.ds(i * GROUP, GROUP)
        return pltpu.make_async_copy(all_ref.at[part], rows_ref.at[part], in_sems.at[i])

    def send(i):
        part = pl.ds(i * GROUP, GROUP)
        return pltpu.make_async_copy(out_ref.at[part], u_ref.at[part], out_sems.at[i])

    for i in range(groups):
        fetch(i).start()
    pivots = scalars[0]
    row = scalars[1]
    lows = [low0_ref[0], low_ref[0], low_ref[1]]
    invs = [inv0_ref[0], inv_ref[0], inv_ref[1]]
    solved, panels = solve_own(own_ref[...], invs, pan_ref)
    for t in range(STEPS):
        active = t < pivots
        block = jnp.where(row > t, solved[t], jnp.where(row == t, lows[t], 0.0))
        factor_ref[:, t * B : (t + 1) * B] = jnp.where(active, block, 0.0)
        mine_ref[:, t * B : (t + 1) * B] = jnp.where(active, panels[t], 0.0).astype(BF16)
        parts_ref[t, 0], parts_ref[t, 1] = split(invs[t])

    def group(i, carry):
        fetch(i).wait()
        a = rows_ref[pl.ds(i * GROUP, GROUP)].reshape(GROUP * B, STEPS * B)
        panels = solve_panels(a, parts_ref, pan_ref)
        other = jnp.concatenate(
            [jnp.where(t < pivots, panels[t], 0.0).astype(BF16) for t in range(STEPS)], axis=1
        )
        for k in range(GROUP):
            half_update(row, i * GROUP + k, mine_ref, other[k * B : (k + 1) * B], out_ref)
        send(i).start()
        return carry

    lax.fori_loop(0, groups, group, 0)
    for i in range(groups):
        send(i).wait()


def solve_and_update(scalars, own, gathered, low0, inv0, low, inv, pan):
    blocks = gathered.shape[0]
    return pl.pallas_call(
        update_kernel,
        in_specs=[pl.BlockSpec(memory_space=pltpu.SMEM), VMEM, ANY] + [VMEM] * 5,
        out_specs=[VMEM, ANY],
        out_shape=[
            jax.ShapeDtypeStruct((B, STEPS * B), F32),
            jax.ShapeDtypeStruct((blocks, H + EXTRA, B), BF16),
        ],
        scratch_shapes=[
            pltpu.VMEM((B, STEPS * B), BF16),
            pltpu.VMEM((STEPS, 2, B, B), BF16),
            pltpu.VMEM((blocks, B, STEPS * B), BF16),
            pltpu.VMEM((blocks, H + EXTRA, B), BF16),
            pltpu.SemaphoreType.DMA((blocks // GROUP,)),
            pltpu.SemaphoreType.DMA((blocks // GROUP,)),
        ],
        compiler_params=pltpu.CompilerParams(vmem_limit_bytes=48 << 20),
        cost_estimate=pl.CostEstimate(
            flops=16_000_000_000, bytes_accessed=10 << 20, transcendentals=0
        ),
    )(scalars, own, gathered, low0, inv0, low, inv, pan)


def relayout_kernel(x_ref, y_ref):
    for i in range(GROUP):
        y_ref[i] = x_ref[:, i * B : (i + 1) * B]


def block_columns(front):
    blocks = front.shape[1] // B
    return pl.pallas_call(
        relayout_kernel,
        grid=(blocks // GROUP,),
        in_specs=[pl.BlockSpec((B, GROUP * B), lambda j: (0, j))],
        out_specs=pl.BlockSpec((GROUP, B, B), lambda j: (j, 0, 0)),
        out_shape=jax.ShapeDtypeStruct((blocks, B, B), front.dtype),
        cost_estimate=pl.CostEstimate(flops=0, bytes_accessed=4 << 20, transcendentals=0),
    )(front)


def start_sum_kernel(slots, x_ref, anc_ref, acc_ref):
    k = pl.program_id(0)

    @pl.when(k == 0)
    def _():
        acc_ref[0:2] = anc_ref[...].astype(F32)
        acc_ref[2:4] = jnp.zeros((2, B, B), F32)

    for i in range(GROUP):
        slot = slots[k * GROUP + i]

        @pl.when(slot < 4)
        def _(i=i, slot=slot):
            acc_ref[slot] += x_ref[i].astype(F32)


def sum_fronts(slots, x, ancestor):
    return pl.pallas_call(
        start_sum_kernel,
        grid=(x.shape[0] // GROUP,),
        in_specs=[
            pl.BlockSpec(memory_space=pltpu.SMEM),
            pl.BlockSpec((GROUP, B, B), lambda k: (k, 0, 0)),
            pl.BlockSpec(ancestor.shape, lambda k: (0, 0, 0)),
        ],
        out_specs=pl.BlockSpec((4, B, B), lambda k: (0, 0, 0)),
        out_shape=jax.ShapeDtypeStruct((4, B, B), F32),
        compiler_params=pltpu.CompilerParams(vmem_limit_bytes=40 << 20),
        cost_estimate=pl.CostEstimate(
            flops=4_000_000_000, bytes_accessed=4 << 20, transcendentals=0
        ),
    )(slots, x, ancestor)


def update_sum_kernel(slots, side_ref, x_ref, own_ref, far_ref, near_mirror, far_mirror, acc_ref):
    k = pl.program_id(0)

    @pl.when(k == 0)
    def _():
        acc_ref[...] = jnp.zeros_like(acc_ref)

    for i in range(GROUP):
        slot = slots[k * GROUP + i]

        @pl.when(slot < 4)
        def _(i=i, slot=slot):
            acc_ref[slot] += x_ref[i].astype(F32)

    @pl.when(k == pl.num_programs(0) - 1)
    def _():
        side = side_ref[0]
        for h in range(2):
            own_ref[h] = acc_ref[2 * side + h]
            far_ref[h] = acc_ref[2 * (1 - side) + h].astype(BF16)
            near_mirror[h] = acc_ref[2 * h + side][:H].astype(BF16)
            far_mirror[h] = acc_ref[2 * h + 1 - side][:H].astype(BF16)


def sum_updates(slots, side, x):
    rows = x.shape[1]
    whole = lambda k: (0, 0, 0)
    return pl.pallas_call(
        update_sum_kernel,
        grid=(x.shape[0] // GROUP,),
        in_specs=[
            pl.BlockSpec(memory_space=pltpu.SMEM),
            pl.BlockSpec(memory_space=pltpu.SMEM),
            pl.BlockSpec((GROUP, rows, B), lambda k: (k, 0, 0)),
        ],
        out_specs=[
            pl.BlockSpec((2, rows, B), whole),
            pl.BlockSpec((2, rows, B), whole),
            pl.BlockSpec((2, H, B), whole),
            pl.BlockSpec((2, H, B), whole),
        ],
        out_shape=[
            jax.ShapeDtypeStruct((2, rows, B), F32),
            jax.ShapeDtypeStruct((2, rows, B), BF16),
            jax.ShapeDtypeStruct((2, H, B), BF16),
            jax.ShapeDtypeStruct((2, H, B), BF16),
        ],
        scratch_shapes=[pltpu.VMEM((4, rows, B), F32)],
        compiler_params=pltpu.CompilerParams(vmem_limit_bytes=40 << 20),
        cost_estimate=pl.CostEstimate(
            flops=2_000_000, bytes_accessed=3 << 20, transcendentals=0
        ),
    )(slots, side, x)


def finish_kernel(place, start_ref, far_start, own_ref, far_ref, mirror_a, mirror_b, out_ref):
    row = place[0]
    block_col = place[1]
    for h in range(2):
        start = start_ref[h] + far_start[h]
        mine = own_ref[h] + far_ref[h].astype(F32)
        mirror = mirror_a[h].astype(F32) + mirror_b[h].astype(F32)

        @pl.when(row < block_col)
        def _(h=h, start=start, mine=mine, mirror=mirror):
            out_ref[h] = start - jnp.concatenate([mine[:H], mirror], axis=0)

        @pl.when(row > block_col)
        def _(h=h, start=start, mine=mine, mirror=mirror):
            out_ref[h] = start - jnp.concatenate([mirror, mine[:H]], axis=0).T

        @pl.when(row == block_col)
        def _(h=h, start=start, mine=mine):
            ri = lax.broadcasted_iota(jnp.int32, (H, H), 0)
            ci = lax.broadcasted_iota(jnp.int32, (H, H), 1)
            packed = mine[:H, :H]
            turned = packed.T
            side = mine[:H, H:]
            first = jnp.where(ri >= ci, packed, turned)
            diagonal = jnp.broadcast_to(mine[H : H + 1, :H], (H, H))
            last = jnp.where(ri < ci, packed, jnp.where(ri > ci, turned, diagonal))
            top = jnp.concatenate([first, side], axis=1)
            bottom = jnp.concatenate([side.T, last], axis=1)
            out_ref[h] = start - jnp.concatenate([top, bottom], axis=0)


def finish(place, *arrays):
    return pl.pallas_call(
        finish_kernel,
        in_specs=[pl.BlockSpec(memory_space=pltpu.SMEM)] + [VMEM] * len(arrays),
        out_specs=VMEM,
        out_shape=jax.ShapeDtypeStruct((2, B, B), F32),
        compiler_params=pltpu.CompilerParams(vmem_limit_bytes=40 << 20),
        cost_estimate=pl.CostEstimate(
            flops=2_000_000, bytes_accessed=3 << 20, transcendentals=0
        ),
    )(place, *arrays)


def broadcast_first(block, row):
    size = lax.axis_size("row")
    step = size // 2
    while step:
        pairs = [(i, i + step) for i in range(0, size, 2 * step)]
        got = lax.ppermute(block, "row", pairs)
        block = jnp.where(row % (2 * step) == step, got, block)
        step //= 2
    return block


def shards(fronts, pivots, targets, ancestor):
    row = lax.axis_index("row")
    col = lax.axis_index("col")
    cols = lax.axis_size("col")
    blocks = fronts.shape[2] // B
    half = cols // 2
    groups = [list(range(half)), list(range(half, cols))]
    front = fronts[0]

    side = col // half
    block_col = col % half
    first = side * half
    piv = lax.dynamic_slice_in_dim(pivots, first, half)
    tgt = lax.dynamic_slice_in_dim(targets, first, half, axis=0)
    col_half = lax.dynamic_index_in_dim(tgt, block_col, 1, keepdims=False) // blocks
    row_half = lax.dynamic_index_in_dim(tgt, row, 1, keepdims=False) // blocks
    keep = (block_col >= piv) & (row >= piv)
    slots = jnp.where(keep, jnp.where(col_half == side, 0, 2) + row_half, 4).astype(jnp.int32)
    update_slots = jnp.where(keep, 2 * col_half + row_half, 4).astype(jnp.int32)
    place = jnp.stack([row, block_col]).astype(jnp.int32)
    far = [(c, (c + half) % cols) for c in range(cols)]
    mirror = [
        [
            ((i * 2 + z) * half + j, (j * 2 + (z + turn) % 2) * half + i)
            for i in range(blocks)
            for z in range(2)
            for j in range(half)
        ]
        for turn in range(2)
    ]
    scalars = jnp.stack([pivots[col], row.astype(jnp.int32)])

    own, corner = lax.optimization_barrier((front[:, : STEPS * B], front[:, :B]))
    gathered = lax.all_gather(own, "row", axis=0, tiled=False)
    corner = broadcast_first(corner, row)
    low0, inv0 = factor_first(corner)
    f = lax.all_to_all(
        block_columns(front), "col", 0, 0, axis_index_groups=groups, tiled=True
    )

    low, inv, pan = factor_rest(gathered[1:STEPS].reshape((STEPS - 1) * B, STEPS * B), inv0)
    start = sum_fronts(slots, f, ancestor)
    far_start, inv = lax.optimization_barrier((start[2:4], inv))
    far_start = lax.ppermute(far_start, "col", far)
    factor, u = solve_and_update(scalars, own, gathered, low0, inv0, low, inv, pan)
    u = lax.all_to_all(u, "col", 0, 0, axis_index_groups=groups, tiled=True)

    own_sum, far_sum, mirror_a, mirror_b = sum_updates(
        update_slots, side.astype(jnp.int32)[None], u
    )
    far_sum = lax.ppermute(far_sum, "col", far)
    mirror_a = lax.ppermute(mirror_a, ("row", "col"), mirror[0])
    mirror_b = lax.ppermute(mirror_b, ("row", "col"), mirror[1])
    out = finish(place, start[0:2], far_start, own_sum, far_sum, mirror_a, mirror_b)
    return factor[None], out


def solution(mesh):
    in_specs = (P("col", "row", None), P(), P(), P(None, "row", "col"))
    out_specs = (P("col", "row", None), P(None, "row", "col"))
    return jax.shard_map(shards, mesh=mesh, in_specs=in_specs, out_specs=out_specs, check_vma=False)
```

```python
import jax
import jax.numpy as jnp
from jax import lax
from jax.experimental import pallas as pl
from jax.experimental.pallas import tpu as pltpu
from jax.sharding import PartitionSpec as P

STEPS = 3
B = 256
SUB = 8
PANEL = 32
GROUP = 4
VMEM = pl.BlockSpec(memory_space=pltpu.VMEM)
ANY = pl.BlockSpec(memory_space=pl.ANY)
F32 = jnp.float32
BF16 = jnp.bfloat16
HIGHEST = lax.Precision.HIGHEST


def dot_nt(a, b, precision=None):
    return lax.dot_general(
        a, b, (((1,), (1,)), ((), ())), precision=precision, preferred_element_type=F32
    )


def wide(v):
    return jnp.concatenate([v, v], axis=1)


def tree_sum(terms):
    terms = list(terms)
    while len(terms) > 1:
        pairs = [terms[i : i + 2] for i in range(0, len(terms), 2)]
        terms = [p[0] + p[1] if len(p) == 2 else p[0] for p in pairs]
    return terms[0]


def small_ldl(e):
    m = [[None] * SUB for _ in range(SUB)]
    rc = [None] * SUB
    for k in range(SUB):
        rc[k] = 1.0 / e[k][k]
        for a in range(k + 1, SUB):
            m[a][k] = e[a][k] * rc[k]
        for a in range(k + 1, SUB):
            for b in range(k + 1, a + 1):
                e[a][b] = e[a][b] - m[a][k] * e[b][k]
    inv = [[None] * SUB for _ in range(SUB)]
    for b in range(SUB):
        for a in range(b + 1, SUB):
            v = m[a][b]
            for c in range(b + 1, a):
                v = v + m[a][c] * inv[c][b]
            inv[a][b] = -v
    return inv, rc, [e[k][k] for k in range(SUB)]


def factor_tiles(tiles, b0):
    count = len(tiles)
    lane = lax.broadcasted_iota(jnp.int32, (SUB, B), 1)
    sub = lax.broadcasted_iota(jnp.int32, (SUB, B), 0)
    narrow = lax.broadcasted_iota(jnp.int32, (SUB, 128), 0)
    tiles = list(tiles)
    keep = []
    update = []
    for i in range(count):
        k0 = b0 + SUB * i
        x = tiles[i]
        e = [[None] * SUB for _ in range(SUB)]
        for a in range(SUB):
            for b in range(a + 1):
                e[a][b] = jnp.broadcast_to(x[a : a + 1, k0 + b : k0 + b + 1], (SUB, 128))
        inv, rc, d = small_ldl(e)
        cols = []
        for b in range(SUB):
            v = jnp.where(narrow == b, 1.0, 0.0)
            for a in range(b + 1, SUB):
                v = jnp.where(narrow == a, inv[a][b], v)
            cols.append(v)
        pivot = d[0]
        for a in range(1, SUB):
            pivot = jnp.where(narrow == a, d[a], pivot)
        scale = wide(lax.rsqrt(pivot))
        r = tree_sum(
            wide(cols[b]) * jnp.broadcast_to(x[b : b + 1, :], (SUB, B)) for b in range(SUB)
        )
        z = 0.0
        for b in range(SUB):
            z = jnp.where(lane == k0 + b, wide(cols[b]), z)
        in_block = (lane >= k0) & (lane < k0 + SUB)
        y = jnp.where(in_block, z, r)
        if i < count - 1:
            rows = []
            for a in range(SUB):
                v = jnp.where(narrow == a, rc[a], 0.0)
                for b in range(a):
                    v = jnp.where(narrow == b, inv[a][b] * rc[a], v)
                rows.append(v)
            g = tree_sum(
                wide(rows[a]) * jnp.broadcast_to(y[a : a + 1, :], (SUB, B)) for a in range(SUB)
            )
            for j in range(i + 1, count):
                t = tiles[j]
                tiles[j] = jnp.where(in_block, 0.0, t) - tree_sum(
                    jnp.broadcast_to(t[:, k0 + b : k0 + b + 1], (SUB, B))
                    * jnp.broadcast_to(g[b : b + 1, :], (SUB, B))
                    for b in range(SUB)
                )
        scaled = y * scale
        keep.append(jnp.where(in_block & (lane > k0 + sub), r * scale, scaled))
        later = (lane >= k0 + SUB) & (lane < b0 + SUB * count)
        update.append(jnp.where(later, 0.0, scaled))
    return keep, update


def cholesky_in_place(t_ref, beside):
    count = PANEL // SUB
    tiles = [t_ref[SUB * i : SUB * (i + 1), :] for i in range(count)]
    for b0 in range(0, B, PANEL):
        b1 = b0 + PANEL
        beside(b0 // PANEL)
        keep, update = factor_tiles(tiles, b0)
        for i in range(count):
            t_ref[b0 + SUB * i : b0 + SUB * (i + 1), :] = keep[i]
        if b1 == B:
            break
        right = jnp.concatenate(update, axis=0)
        left = right.T

        def below(lo, hi):
            lanes = lax.broadcasted_iota(jnp.int32, (hi - lo, B), 1)
            old = jnp.where((lanes >= b0) & (lanes < b1), 0.0, t_ref[lo:hi, :])
            return old - jnp.dot(
                left[lo:hi], right, precision=HIGHEST, preferred_element_type=F32
            )

        ahead = below(b1, b1 + PANEL)
        tiles = [ahead[SUB * i : SUB * (i + 1), :] for i in range(count)]
        if b1 + PANEL < B:
            t_ref[b1 + PANEL :, :] = below(b1 + PANEL, B)


def factor_block(d, t_ref, beside=lambda q: None):
    t_ref[...] = 0.5 * (d + d.T)
    cholesky_in_place(t_ref, beside)
    t = t_ref[...]
    ri = lax.broadcasted_iota(jnp.int32, (B, B), 0)
    ci = lax.broadcasted_iota(jnp.int32, (B, B), 1)
    inv = jnp.where(ci <= ri, t, 0.0)
    low = jnp.where(ci > ri, t, jnp.where(ci == ri, 1.0 / t, 0.0)).T
    return low, inv


def first_kernel(a_ref, low_ref, inv_ref, t_ref):
    low_ref[...], inv_ref[...] = factor_block(a_ref[...].astype(F32), t_ref)


def factor_first(block):
    return pl.pallas_call(
        first_kernel,
        in_specs=[VMEM],
        out_specs=[VMEM, VMEM],
        out_shape=[jax.ShapeDtypeStruct((B, B), F32)] * 2,
        scratch_shapes=[pltpu.VMEM((B, B), F32)],
        compiler_params=pltpu.CompilerParams(vmem_limit_bytes=40 << 20),
        cost_estimate=pl.CostEstimate(
            flops=10_000_000_000, bytes_accessed=1 << 20, transcendentals=0
        ),
    )(block)


def split(x):
    high = x.astype(BF16)
    return high, (x - high.astype(F32)).astype(BF16)


def rest_kernel(
    scalars,
    own_ref,
    all_ref,
    low0_ref,
    inv0_ref,
    factor_ref,
    u_ref,
    rows_ref,
    corner_ref,
    t_ref,
    mine_ref,
    mine_rest,
    parts_ref,
    pan_ref,
    p_ref,
    high_ref,
    low_part_ref,
    sum_ref,
    out_ref,
    in_sems,
    out_sems,
):
    blocks = u_ref.shape[0]
    groups = blocks // GROUP
    per_panel = blocks // (B // PANEL)
    pivots = scalars[0]
    row = scalars[1]

    def fetch(i):
        part = pl.ds(i * GROUP, GROUP)
        return pltpu.make_async_copy(all_ref.at[part], rows_ref.at[part], in_sems.at[i])

    def send(i):
        part = pl.ds(i * GROUP, GROUP)
        return pltpu.make_async_copy(out_ref.at[part], u_ref.at[part], out_sems.at[i])

    def cols(t):
        return slice(t * B, (t + 1) * B)

    def take_inverse(t, inv):
        parts_ref[t, 0], parts_ref[t, 1] = split(inv)

    def own_step(t, w, low, inv):
        solved = dot_nt(w, inv, HIGHEST)
        block = jnp.where(row > t, solved, jnp.where(row == t, low, 0.0))
        factor_ref[:, cols(t)] = jnp.where(t < pivots, block, 0.0)
        panel = solved.astype(BF16)
        mine_ref[:, cols(t)] = jnp.where(t < pivots, panel, 0.0).astype(BF16)
        return panel

    def other_step(t, j):
        high, low = parts_ref[t, 0], parts_ref[t, 1]
        if t == 0:
            a = rows_ref[j, :, cols(0)]
            x = dot_nt(a, high) + dot_nt(a, low)
        else:
            wh, wl = high_ref[j], low_part_ref[j]
            x = dot_nt(wh, high) + (dot_nt(wl, high) + dot_nt(wh, low))
        return x.astype(BF16)

    for i in range(groups):
        fetch(i).start()
    inv0 = inv0_ref[...]
    take_inverse(0, inv0)
    fetch(0).wait()

    p1 = dot_nt(rows_ref[1, :, cols(0)].astype(F32), inv0, HIGHEST).astype(BF16)
    p2 = dot_nt(rows_ref[2, :, cols(0)].astype(F32), inv0, HIGHEST).astype(BF16)
    pan_ref[0] = p1
    pan_ref[1] = p2
    d = rows_ref[1, :, cols(1)].astype(F32) - dot_nt(p1, p1)
    corner_ref[0] = rows_ref[2, :, cols(1)].astype(F32) - dot_nt(p2, p1)
    corner_ref[1] = rows_ref[2, :, cols(2)].astype(F32) - dot_nt(p2, p2)

    def beside_first(q):
        if q == 0:
            panel = own_step(0, own_ref[:, cols(0)].astype(F32), low0_ref[...], inv0)
            mine_rest[0] = own_ref[:, cols(1)].astype(F32) - dot_nt(panel, pan_ref[0])
            mine_rest[1] = own_ref[:, cols(2)].astype(F32) - dot_nt(panel, pan_ref[1])
        for j in range(q * per_panel, (q + 1) * per_panel):
            if j and j % GROUP == 0:
                fetch(j // GROUP).wait()
            p = other_step(0, j)
            p_ref[j] = p
            w = rows_ref[j, :, cols(1)].astype(F32) - dot_nt(p, pan_ref[0])
            high_ref[j], low_part_ref[j] = split(w)

    low1, inv1 = factor_block(d, t_ref, beside_first)
    take_inverse(1, inv1)

    p21 = dot_nt(corner_ref[0], inv1, HIGHEST).astype(BF16)
    pan_ref[2] = p21
    d = corner_ref[1] - dot_nt(p21, p21)

    def beside_second(q):
        if q == 0:
            panel = own_step(1, mine_rest[0], low1, inv1)
            mine_rest[1] = mine_rest[1] - dot_nt(panel, pan_ref[2])
        for j in range(q * per_panel, (q + 1) * per_panel):
            p0 = p_ref[j]
            p1 = other_step(1, j)
            w = rows_ref[j, :, cols(2)].astype(F32)
            w = w - dot_nt(p0, pan_ref[1]) - dot_nt(p1, pan_ref[2])
            high_ref[j], low_part_ref[j] = split(w)
            p1 = jnp.where(1 < pivots, p1, 0.0).astype(BF16)
            sum_ref[j] = dot_nt(mine_ref[:, cols(0)], p0) + dot_nt(mine_ref[:, cols(1)], p1)

    low2, inv2 = factor_block(d, t_ref, beside_second)
    take_inverse(2, inv2)
    own_step(2, mine_rest[1], low2, inv2)

    def last(i, carry):
        for k in range(GROUP):
            j = i * GROUP + k
            p2 = jnp.where(2 < pivots, other_step(2, j), 0.0).astype(BF16)
            out_ref[j] = (sum_ref[j] + dot_nt(mine_ref[:, cols(2)], p2)).astype(BF16)
        send(i).start()
        return carry

    lax.fori_loop(0, groups, last, 0)
    for i in range(groups):
        send(i).wait()


def factor_and_update(scalars, own, gathered, low0, inv0):
    blocks = gathered.shape[0]
    return pl.pallas_call(
        rest_kernel,
        in_specs=[pl.BlockSpec(memory_space=pltpu.SMEM), VMEM, ANY, VMEM, VMEM],
        out_specs=[VMEM, pl.BlockSpec(memory_space=pltpu.HBM)],
        out_shape=[
            jax.ShapeDtypeStruct((B, STEPS * B), F32),
            jax.ShapeDtypeStruct((blocks, B, B), BF16),
        ],
        scratch_shapes=[
            pltpu.VMEM((blocks, B, STEPS * B), BF16),
            pltpu.VMEM((2, B, B), F32),
            pltpu.VMEM((B, B), F32),
            pltpu.VMEM((B, STEPS * B), BF16),
            pltpu.VMEM((2, B, B), F32),
            pltpu.VMEM((STEPS, 2, B, B), BF16),
            pltpu.VMEM((STEPS, B, B), BF16),
            pltpu.VMEM((blocks, B, B), BF16),
            pltpu.VMEM((blocks, B, B), BF16),
            pltpu.VMEM((blocks, B, B), BF16),
            pltpu.VMEM((blocks, B, B), F32),
            pltpu.VMEM((blocks, B, B), BF16),
            pltpu.SemaphoreType.DMA((blocks // GROUP,)),
            pltpu.SemaphoreType.DMA((blocks // GROUP,)),
        ],
        compiler_params=pltpu.CompilerParams(vmem_limit_bytes=48 << 20),
        cost_estimate=pl.CostEstimate(
            flops=30_000_000_000, bytes_accessed=10 << 20, transcendentals=0
        ),
    )(scalars, own, gathered, low0, inv0)


def relayout_kernel(x_ref, y_ref):
    for i in range(GROUP):
        y_ref[i] = x_ref[:, i * B : (i + 1) * B]


def block_columns(front):
    blocks = front.shape[1] // B
    return pl.pallas_call(
        relayout_kernel,
        grid=(blocks // GROUP,),
        in_specs=[pl.BlockSpec((B, GROUP * B), lambda j: (0, j))],
        out_specs=pl.BlockSpec((GROUP, B, B), lambda j: (j, 0, 0)),
        out_shape=jax.ShapeDtypeStruct((blocks, B, B), front.dtype),
        cost_estimate=pl.CostEstimate(flops=0, bytes_accessed=4 << 20, transcendentals=0),
    )(front)


def start_sum_kernel(slots, x_ref, anc_ref, acc_ref):
    k = pl.program_id(0)

    @pl.when(k == 0)
    def _():
        acc_ref[0:2] = anc_ref[...].astype(F32)
        acc_ref[2:4] = jnp.zeros((2, B, B), F32)

    for i in range(GROUP):
        slot = slots[k * GROUP + i]

        @pl.when(slot < 4)
        def _(i=i, slot=slot):
            acc_ref[slot] += x_ref[i].astype(F32)


def end_sum_kernel(slots, x_ref, start_ref, far_ref, own_ref, send_ref, acc_ref):
    k = pl.program_id(0)

    @pl.when(k == 0)
    def _():
        acc_ref[0:2] = start_ref[0:2] + far_ref[...]
        acc_ref[2:4] = jnp.zeros((2, B, B), F32)

    for i in range(GROUP):
        slot = slots[k * GROUP + i]

        @pl.when(slot < 4)
        def _(i=i, slot=slot):
            acc_ref[slot] -= x_ref[i].astype(F32)

    @pl.when(k == pl.num_programs(0) - 1)
    def _():
        own_ref[...] = acc_ref[0:2]
        send_ref[...] = acc_ref[2:4].astype(BF16)


def sum_fronts(slots, x, ancestor):
    return pl.pallas_call(
        start_sum_kernel,
        grid=(x.shape[0] // GROUP,),
        in_specs=[
            pl.BlockSpec(memory_space=pltpu.SMEM),
            pl.BlockSpec((GROUP, B, B), lambda k: (k, 0, 0)),
            pl.BlockSpec((2, B, B), lambda k: (0, 0, 0)),
        ],
        out_specs=pl.BlockSpec((4, B, B), lambda k: (0, 0, 0)),
        out_shape=jax.ShapeDtypeStruct((4, B, B), F32),
        compiler_params=pltpu.CompilerParams(vmem_limit_bytes=40 << 20),
        cost_estimate=pl.CostEstimate(
            flops=4_000_000, bytes_accessed=4 << 20, transcendentals=0
        ),
    )(slots, x, ancestor)


def sum_updates(slots, x, start, far):
    return pl.pallas_call(
        end_sum_kernel,
        grid=(x.shape[0] // GROUP,),
        in_specs=[
            pl.BlockSpec(memory_space=pltpu.SMEM),
            pl.BlockSpec((GROUP, B, B), lambda k: (k, 0, 0)),
            pl.BlockSpec((4, B, B), lambda k: (0, 0, 0)),
            pl.BlockSpec((2, B, B), lambda k: (0, 0, 0)),
        ],
        out_specs=[pl.BlockSpec((2, B, B), lambda k: (0, 0, 0))] * 2,
        out_shape=[
            jax.ShapeDtypeStruct((2, B, B), F32),
            jax.ShapeDtypeStruct((2, B, B), BF16),
        ],
        scratch_shapes=[pltpu.VMEM((4, B, B), F32)],
        compiler_params=pltpu.CompilerParams(vmem_limit_bytes=40 << 20),
        cost_estimate=pl.CostEstimate(
            flops=4_000_000, bytes_accessed=4 << 20, transcendentals=0
        ),
    )(slots, x, start, far)


def broadcast_first(block, row):
    size = lax.axis_size("row")
    step = size // 2
    while step:
        pairs = [(i, i + step) for i in range(0, size, 2 * step)]
        got = lax.ppermute(block, "row", pairs)
        block = jnp.where(row % (2 * step) == step, got, block)
        step //= 2
    return block


def shards(fronts, pivots, targets, ancestor):
    row = lax.axis_index("row")
    col = lax.axis_index("col")
    cols = lax.axis_size("col")
    blocks = fronts.shape[2] // B
    half = cols // 2
    groups = [list(range(half)), list(range(half, cols))]
    front = fronts[0]

    side = col // half
    block_col = col % half
    first = side * half
    piv = lax.dynamic_slice_in_dim(pivots, first, half)
    tgt = lax.dynamic_slice_in_dim(targets, first, half, axis=0)
    col_half = lax.dynamic_index_in_dim(tgt, block_col, 1, keepdims=False) // blocks
    row_half = lax.dynamic_index_in_dim(tgt, row, 1, keepdims=False) // blocks
    keep = (block_col >= piv) & (row >= piv)
    slots = jnp.where(keep, jnp.where(col_half == side, 0, 2) + row_half, 4).astype(jnp.int32)
    scalars = jnp.stack([pivots[col], row.astype(jnp.int32)])

    own, corner = lax.optimization_barrier((front[:, : STEPS * B], front[:, :B]))
    gathered = lax.all_gather(own, "row", axis=0, tiled=False)
    corner = broadcast_first(corner, row)
    low0, inv0 = factor_first(corner)
    f = lax.all_to_all(
        block_columns(front), "col", 0, 0, axis_index_groups=groups, tiled=True
    )

    far = [(c, (c + half) % cols) for c in range(cols)]
    start = sum_fronts(slots, f, ancestor)
    sent, gathered = lax.optimization_barrier((start[2:4], gathered))
    received = lax.ppermute(sent, "col", far)
    factor, u = factor_and_update(scalars, own, gathered, low0, inv0)
    received, u = lax.optimization_barrier((received, u))
    u = lax.all_to_all(u, "col", 0, 0, axis_index_groups=groups, tiled=True)

    mine, sent = sum_updates(slots, u, start, received)
    received = lax.ppermute(sent, "col", far)
    return factor[None], mine + received.astype(F32)


def solution(mesh):
    in_specs = (P("col", "row", None), P(), P(), P(None, "row", "col"))
    out_specs = (P("col", "row", None), P(None, "row", "col"))
    return jax.shard_map(shards, mesh=mesh, in_specs=in_specs, out_specs=out_specs, check_vma=False)
```

```python
import jax
import jax.numpy as jnp
from jax import lax
from jax.experimental import pallas as pl
from jax.experimental.pallas import tpu as pltpu
from jax.sharding import PartitionSpec as P

STEPS = 3
B = 256
SUB = 8
PANEL = 32
GROUP = 4
H = B // 2
VMEM = pl.BlockSpec(memory_space=pltpu.VMEM)
ANY = pl.BlockSpec(memory_space=pl.ANY)
F32 = jnp.float32
BF16 = jnp.bfloat16
HIGHEST = lax.Precision.HIGHEST


def dot_nt(a, b, precision=None):
    return lax.dot_general(
        a, b, (((1,), (1,)), ((), ())), precision=precision, preferred_element_type=F32
    )


def wide(v):
    return jnp.concatenate([v, v], axis=1)


def tree_sum(terms):
    terms = list(terms)
    while len(terms) > 1:
        pairs = [terms[i : i + 2] for i in range(0, len(terms), 2)]
        terms = [p[0] + p[1] if len(p) == 2 else p[0] for p in pairs]
    return terms[0]


def small_ldl(e):
    m = [[None] * SUB for _ in range(SUB)]
    rc = [None] * SUB
    for k in range(SUB):
        rc[k] = 1.0 / e[k][k]
        for a in range(k + 1, SUB):
            m[a][k] = e[a][k] * rc[k]
        for a in range(k + 1, SUB):
            for b in range(k + 1, a + 1):
                e[a][b] = e[a][b] - m[a][k] * e[b][k]
    inv = [[None] * SUB for _ in range(SUB)]
    for b in range(SUB):
        for a in range(b + 1, SUB):
            v = m[a][b]
            for c in range(b + 1, a):
                v = v + m[a][c] * inv[c][b]
            inv[a][b] = -v
    return inv, rc, [e[k][k] for k in range(SUB)]


def factor_tiles(tiles, b0):
    count = len(tiles)
    lane = lax.broadcasted_iota(jnp.int32, (SUB, B), 1)
    sub = lax.broadcasted_iota(jnp.int32, (SUB, B), 0)
    narrow = lax.broadcasted_iota(jnp.int32, (SUB, 128), 0)
    tiles = list(tiles)
    keep = []
    update = []
    for i in range(count):
        k0 = b0 + SUB * i
        x = tiles[i]
        e = [[None] * SUB for _ in range(SUB)]
        for a in range(SUB):
            for b in range(a + 1):
                e[a][b] = jnp.broadcast_to(x[a : a + 1, k0 + b : k0 + b + 1], (SUB, 128))
        inv, rc, d = small_ldl(e)
        cols = []
        for b in range(SUB):
            v = jnp.where(narrow == b, 1.0, 0.0)
            for a in range(b + 1, SUB):
                v = jnp.where(narrow == a, inv[a][b], v)
            cols.append(v)
        pivot = d[0]
        for a in range(1, SUB):
            pivot = jnp.where(narrow == a, d[a], pivot)
        scale = wide(lax.rsqrt(pivot))
        r = tree_sum(
            wide(cols[b]) * jnp.broadcast_to(x[b : b + 1, :], (SUB, B)) for b in range(SUB)
        )
        z = 0.0
        for b in range(SUB):
            z = jnp.where(lane == k0 + b, wide(cols[b]), z)
        in_block = (lane >= k0) & (lane < k0 + SUB)
        y = jnp.where(in_block, z, r)
        if i < count - 1:
            rows = []
            for a in range(SUB):
                v = jnp.where(narrow == a, rc[a], 0.0)
                for b in range(a):
                    v = jnp.where(narrow == b, inv[a][b] * rc[a], v)
                rows.append(v)
            g = tree_sum(
                wide(rows[a]) * jnp.broadcast_to(y[a : a + 1, :], (SUB, B)) for a in range(SUB)
            )
            for j in range(i + 1, count):
                t = tiles[j]
                tiles[j] = jnp.where(in_block, 0.0, t) - tree_sum(
                    jnp.broadcast_to(t[:, k0 + b : k0 + b + 1], (SUB, B))
                    * jnp.broadcast_to(g[b : b + 1, :], (SUB, B))
                    for b in range(SUB)
                )
        scaled = y * scale
        keep.append(jnp.where(in_block & (lane > k0 + sub), r * scale, scaled))
        later = (lane >= k0 + SUB) & (lane < b0 + SUB * count)
        update.append(jnp.where(later, 0.0, scaled))
    return keep, update


def cholesky_in_place(t_ref, beside):
    count = PANEL // SUB
    tiles = [t_ref[SUB * i : SUB * (i + 1), :] for i in range(count)]
    for b0 in range(0, B, PANEL):
        b1 = b0 + PANEL
        beside(b0 // PANEL)
        keep, update = factor_tiles(tiles, b0)
        for i in range(count):
            t_ref[b0 + SUB * i : b0 + SUB * (i + 1), :] = keep[i]
        if b1 == B:
            break
        right = jnp.concatenate(update, axis=0)
        left = right.T

        def below(lo, hi):
            lanes = lax.broadcasted_iota(jnp.int32, (hi - lo, B), 1)
            old = jnp.where((lanes >= b0) & (lanes < b1), 0.0, t_ref[lo:hi, :])
            return old - jnp.dot(
                left[lo:hi], right, precision=HIGHEST, preferred_element_type=F32
            )

        ahead = below(b1, b1 + PANEL)
        tiles = [ahead[SUB * i : SUB * (i + 1), :] for i in range(count)]
        if b1 + PANEL < B:
            t_ref[b1 + PANEL :, :] = below(b1 + PANEL, B)


def factor_block(d, t_ref, beside=lambda q: None):
    t_ref[...] = 0.5 * (d + d.T)
    cholesky_in_place(t_ref, beside)
    t = t_ref[...]
    ri = lax.broadcasted_iota(jnp.int32, (B, B), 0)
    ci = lax.broadcasted_iota(jnp.int32, (B, B), 1)
    inv = jnp.where(ci <= ri, t, 0.0)
    low = jnp.where(ci > ri, t, jnp.where(ci == ri, 1.0 / t, 0.0)).T
    return low, inv


def first_kernel(a_ref, low_ref, inv_ref, t_ref):
    low_ref[...], inv_ref[...] = factor_block(a_ref[...].astype(F32), t_ref)


def factor_first(block):
    return pl.pallas_call(
        first_kernel,
        in_specs=[VMEM],
        out_specs=[VMEM, VMEM],
        out_shape=[jax.ShapeDtypeStruct((B, B), F32)] * 2,
        scratch_shapes=[pltpu.VMEM((B, B), F32)],
        compiler_params=pltpu.CompilerParams(vmem_limit_bytes=40 << 20),
        cost_estimate=pl.CostEstimate(
            flops=10_000_000_000, bytes_accessed=1 << 20, transcendentals=0
        ),
    )(block)


def split(x):
    high = x.astype(BF16)
    return high, (x - high.astype(F32)).astype(BF16)


def rest_kernel(
    scalars,
    own_ref,
    all_ref,
    low0_ref,
    inv0_ref,
    factor_ref,
    top_ref,
    bottom_ref,
    rows_ref,
    corner_ref,
    t_ref,
    mine_ref,
    mine_rest,
    parts_ref,
    pan_ref,
    p_ref,
    high_ref,
    low_part_ref,
    sum_ref,
    out_ref,
    in_sems,
    out_sems,
):
    blocks = top_ref.shape[0]
    groups = blocks // GROUP
    per_panel = blocks // (B // PANEL)
    pivots = scalars[0]
    row = scalars[1]

    def fetch(i):
        part = pl.ds(i * GROUP, GROUP)
        return pltpu.make_async_copy(all_ref.at[part], rows_ref.at[part], in_sems.at[i])

    def send(i, half):
        part = pl.ds(i * GROUP, GROUP)
        target = bottom_ref if half else top_ref
        return pltpu.make_async_copy(
            out_ref.at[half, part], target.at[part], out_sems.at[half, i]
        )

    def cols(t):
        return slice(t * B, (t + 1) * B)

    def take_inverse(t, inv):
        parts_ref[t, 0], parts_ref[t, 1] = split(inv)

    def own_step(t, w, low, inv):
        solved = dot_nt(w, inv, HIGHEST)
        block = jnp.where(row > t, solved, jnp.where(row == t, low, 0.0))
        factor_ref[:, cols(t)] = jnp.where(t < pivots, block, 0.0)
        panel = solved.astype(BF16)
        mine_ref[:, cols(t)] = jnp.where(t < pivots, panel, 0.0).astype(BF16)
        return panel

    def other_step(t, j):
        high, low = parts_ref[t, 0], parts_ref[t, 1]
        if t == 0:
            a = rows_ref[j, :, cols(0)]
            x = dot_nt(a, high) + dot_nt(a, low)
        else:
            wh, wl = high_ref[j], low_part_ref[j]
            x = dot_nt(wh, high) + (dot_nt(wl, high) + dot_nt(wh, low))
        return x.astype(BF16)

    for i in range(groups):
        fetch(i).start()
    inv0 = inv0_ref[...]
    take_inverse(0, inv0)
    fetch(0).wait()

    p1 = dot_nt(rows_ref[1, :, cols(0)].astype(F32), inv0, HIGHEST).astype(BF16)
    p2 = dot_nt(rows_ref[2, :, cols(0)].astype(F32), inv0, HIGHEST).astype(BF16)
    pan_ref[0] = p1
    pan_ref[1] = p2
    d = rows_ref[1, :, cols(1)].astype(F32) - dot_nt(p1, p1)
    corner_ref[0] = rows_ref[2, :, cols(1)].astype(F32) - dot_nt(p2, p1)
    corner_ref[1] = rows_ref[2, :, cols(2)].astype(F32) - dot_nt(p2, p2)

    def beside_first(q):
        if q == 0:
            panel = own_step(0, own_ref[:, cols(0)].astype(F32), low0_ref[...], inv0)
            mine_rest[0] = own_ref[:, cols(1)].astype(F32) - dot_nt(panel, pan_ref[0])
            mine_rest[1] = own_ref[:, cols(2)].astype(F32) - dot_nt(panel, pan_ref[1])
        for j in range(q * per_panel, (q + 1) * per_panel):
            if j and j % GROUP == 0:
                fetch(j // GROUP).wait()
            p = other_step(0, j)
            p_ref[j] = p
            w = rows_ref[j, :, cols(1)].astype(F32) - dot_nt(p, pan_ref[0])
            high_ref[j], low_part_ref[j] = split(w)

    low1, inv1 = factor_block(d, t_ref, beside_first)
    take_inverse(1, inv1)

    p21 = dot_nt(corner_ref[0], inv1, HIGHEST).astype(BF16)
    pan_ref[2] = p21
    d = corner_ref[1] - dot_nt(p21, p21)

    def beside_second(q):
        if q == 0:
            panel = own_step(1, mine_rest[0], low1, inv1)
            mine_rest[1] = mine_rest[1] - dot_nt(panel, pan_ref[2])
        for j in range(q * per_panel, (q + 1) * per_panel):
            p0 = p_ref[j]
            p1 = other_step(1, j)
            w = rows_ref[j, :, cols(2)].astype(F32)
            w = w - dot_nt(p0, pan_ref[1]) - dot_nt(p1, pan_ref[2])
            high_ref[j], low_part_ref[j] = split(w)
            p1 = jnp.where(1 < pivots, p1, 0.0).astype(BF16)
            sum_ref[j] = dot_nt(mine_ref[:, cols(0)], p0) + dot_nt(mine_ref[:, cols(1)], p1)

    low2, inv2 = factor_block(d, t_ref, beside_second)
    take_inverse(2, inv2)
    own_step(2, mine_rest[1], low2, inv2)

    def last(i, carry):
        part = pl.ds(i * GROUP, GROUP)
        wh = high_ref[part].reshape(GROUP * B, B)
        wl = low_part_ref[part].reshape(GROUP * B, B)
        high, low = parts_ref[2, 0], parts_ref[2, 1]
        x = dot_nt(wh, high) + (dot_nt(wl, high) + dot_nt(wh, low))
        p2 = jnp.where(2 < pivots, x.astype(BF16), 0.0).astype(BF16)
        for k in range(GROUP):
            j = i * GROUP + k
            product = dot_nt(mine_ref[:, cols(2)], p2[k * B : (k + 1) * B])
            u = (sum_ref[j] + product).astype(BF16)
            out_ref[0, j] = u[:H]
            out_ref[1, j] = u[H:]
        send(i, 0).start()
        send(i, 1).start()
        return carry

    lax.fori_loop(0, groups, last, 0)
    for i in range(groups):
        send(i, 0).wait()
        send(i, 1).wait()


def factor_and_update(scalars, own, gathered, low0, inv0):
    blocks = gathered.shape[0]
    return pl.pallas_call(
        rest_kernel,
        in_specs=[pl.BlockSpec(memory_space=pltpu.SMEM), VMEM, ANY, VMEM, VMEM],
        out_specs=[VMEM] + [pl.BlockSpec(memory_space=pltpu.HBM)] * 2,
        out_shape=[
            jax.ShapeDtypeStruct((B, STEPS * B), F32),
            jax.ShapeDtypeStruct((blocks, H, B), BF16),
            jax.ShapeDtypeStruct((blocks, H, B), BF16),
        ],
        scratch_shapes=[
            pltpu.VMEM((blocks, B, STEPS * B), BF16),
            pltpu.VMEM((2, B, B), F32),
            pltpu.VMEM((B, B), F32),
            pltpu.VMEM((B, STEPS * B), BF16),
            pltpu.VMEM((2, B, B), F32),
            pltpu.VMEM((STEPS, 2, B, B), BF16),
            pltpu.VMEM((STEPS, B, B), BF16),
            pltpu.VMEM((blocks, B, B), BF16),
            pltpu.VMEM((blocks, B, B), BF16),
            pltpu.VMEM((blocks, B, B), BF16),
            pltpu.VMEM((blocks, B, B), F32),
            pltpu.VMEM((2, blocks, H, B), BF16),
            pltpu.SemaphoreType.DMA((blocks // GROUP,)),
            pltpu.SemaphoreType.DMA((2, blocks // GROUP)),
        ],
        compiler_params=pltpu.CompilerParams(vmem_limit_bytes=48 << 20),
        cost_estimate=pl.CostEstimate(
            flops=30_000_000_000, bytes_accessed=10 << 20, transcendentals=0
        ),
    )(scalars, own, gathered, low0, inv0)


def relayout_kernel(x_ref, y_ref):
    for i in range(GROUP):
        y_ref[i] = x_ref[:, i * B : (i + 1) * B]


def block_columns(front):
    blocks = front.shape[1] // B
    return pl.pallas_call(
        relayout_kernel,
        grid=(blocks // GROUP,),
        in_specs=[pl.BlockSpec((B, GROUP * B), lambda j: (0, j))],
        out_specs=pl.BlockSpec((GROUP, B, B), lambda j: (j, 0, 0)),
        out_shape=jax.ShapeDtypeStruct((blocks, B, B), front.dtype),
        cost_estimate=pl.CostEstimate(flops=0, bytes_accessed=4 << 20, transcendentals=0),
    )(front)


def start_sum_kernel(slots, x_ref, anc_ref, acc_ref):
    k = pl.program_id(0)

    @pl.when(k == 0)
    def _():
        acc_ref[0:2] = anc_ref[...].astype(F32)
        acc_ref[2:4] = jnp.zeros((2, B, B), F32)

    for i in range(GROUP):
        slot = slots[k * GROUP + i]

        @pl.when(slot < 4)
        def _(i=i, slot=slot):
            acc_ref[slot] += x_ref[i].astype(F32)


def end_sum_kernel(slots, x_ref, start_ref, own_ref, send_ref, acc_ref):
    k = pl.program_id(0)

    @pl.when(k == 0)
    def _():
        acc_ref[...] = start_ref[...]

    for i in range(GROUP):
        slot = slots[k * GROUP + i]

        @pl.when(slot < 4)
        def _(i=i, slot=slot):
            acc_ref[slot] -= x_ref[i].astype(F32)

    @pl.when(k == pl.num_programs(0) - 1)
    def _():
        own_ref[...] = acc_ref[0:2]
        send_ref[...] = acc_ref[2:4]


def sum_fronts(slots, x, ancestor):
    return pl.pallas_call(
        start_sum_kernel,
        grid=(x.shape[0] // GROUP,),
        in_specs=[
            pl.BlockSpec(memory_space=pltpu.SMEM),
            pl.BlockSpec((GROUP, B, B), lambda k: (k, 0, 0)),
            pl.BlockSpec((2, B, B), lambda k: (0, 0, 0)),
        ],
        out_specs=pl.BlockSpec((4, B, B), lambda k: (0, 0, 0)),
        out_shape=jax.ShapeDtypeStruct((4, B, B), F32),
        compiler_params=pltpu.CompilerParams(vmem_limit_bytes=40 << 20),
        cost_estimate=pl.CostEstimate(
            flops=4_000_000, bytes_accessed=4 << 20, transcendentals=0
        ),
    )(slots, x, ancestor)


def sum_updates(slots, x, start, half):
    return pl.pallas_call(
        end_sum_kernel,
        grid=(x.shape[0] // GROUP,),
        in_specs=[
            pl.BlockSpec(memory_space=pltpu.SMEM),
            pl.BlockSpec((GROUP, H, B), lambda k: (k, 0, 0)),
            pl.BlockSpec((4, H, B), lambda k: (0, half, 0)),
        ],
        out_specs=[pl.BlockSpec((2, H, B), lambda k: (0, 0, 0))] * 2,
        out_shape=[jax.ShapeDtypeStruct((2, H, B), F32)] * 2,
        scratch_shapes=[pltpu.VMEM((4, H, B), F32)],
        compiler_params=pltpu.CompilerParams(vmem_limit_bytes=40 << 20),
        cost_estimate=pl.CostEstimate(
            flops=4_000_000, bytes_accessed=2 << 20, transcendentals=0
        ),
    )(slots, x, start)


def broadcast_first(block, row):
    size = lax.axis_size("row")
    step = size // 2
    while step:
        pairs = [(i, i + step) for i in range(0, size, 2 * step)]
        got = lax.ppermute(block, "row", pairs)
        block = jnp.where(row % (2 * step) == step, got, block)
        step //= 2
    return block


def shards(fronts, pivots, targets, ancestor):
    row = lax.axis_index("row")
    col = lax.axis_index("col")
    cols = lax.axis_size("col")
    blocks = fronts.shape[2] // B
    half = cols // 2
    quarter = half // 2
    lines = [list(range(half)), list(range(half, cols))]
    shifted = [
        list(range(quarter)) + list(range(half + quarter, cols)),
        list(range(half, half + quarter)) + list(range(quarter, half)),
    ]
    front = fronts[0]

    side = col // half
    block_col = col % half
    classes = jnp.arange(half, dtype=jnp.int32)

    def slots_of(upper):
        piv = jnp.where(upper, pivots[half:], pivots[:half])
        tgt = jnp.where(upper[:, None], targets[half:], targets[:half])
        col_half = lax.dynamic_index_in_dim(tgt, block_col, 1, keepdims=False) // blocks
        row_half = lax.dynamic_index_in_dim(tgt, row, 1, keepdims=False) // blocks
        keep = (block_col >= piv) & (row >= piv)
        return jnp.where(keep, jnp.where(col_half == side, 0, 2) + row_half, 4).astype(jnp.int32)

    line_slots = slots_of(jnp.broadcast_to(side == 1, (half,)))
    first_shifted = (col < quarter) | (col >= half + quarter)
    shifted_slots = slots_of((classes >= quarter) == first_shifted)
    scalars = jnp.stack([pivots[col], row.astype(jnp.int32)])

    own, corner = lax.optimization_barrier((front[:, : STEPS * B], front[:, :B]))
    gathered = lax.all_gather(own, "row", axis=0, tiled=False)
    corner = broadcast_first(corner, row)
    low0, inv0 = factor_first(corner)
    f = lax.all_to_all(block_columns(front), "col", 0, 0, axis_index_groups=lines, tiled=True)
    start = sum_fronts(line_slots, f, ancestor)

    factor, top, bottom = factor_and_update(scalars, own, gathered, low0, inv0)
    top = lax.all_to_all(top, "col", 0, 0, axis_index_groups=lines, tiled=True)
    bottom = lax.all_to_all(bottom, "col", 0, 0, axis_index_groups=shifted, tiled=True)

    far = [(c, (c + half) % cols) for c in range(cols)]
    top, top_sent = sum_updates(line_slots, top, start, 0)
    bottom, bottom_sent = sum_updates(shifted_slots, bottom, start, 1)
    top = top + lax.ppermute(top_sent, "col", far)
    bottom = bottom + lax.ppermute(bottom_sent, "col", far)
    return factor[None], jnp.concatenate([top, bottom], axis=1)


def solution(mesh):
    in_specs = (P("col", "row", None), P(), P(), P(None, "row", "col"))
    out_specs = (P("col", "row", None), P(None, "row", "col"))
    return jax.shard_map(shards, mesh=mesh, in_specs=in_specs, out_specs=out_specs, check_vma=False)
```

```python
import jax
import jax.numpy as jnp
from jax import lax
from jax.experimental import pallas as pl
from jax.experimental.pallas import tpu as pltpu
from jax.sharding import PartitionSpec as P

STEPS = 3
B = 256
SUB = 8
PANEL = 32
GROUP = 4
VMEM = pl.BlockSpec(memory_space=pltpu.VMEM)
ANY = pl.BlockSpec(memory_space=pl.ANY)
F32 = jnp.float32
BF16 = jnp.bfloat16
HIGHEST = lax.Precision.HIGHEST


def dot_nt(a, b, precision=None):
    return lax.dot_general(
        a, b, (((1,), (1,)), ((), ())), precision=precision, preferred_element_type=F32
    )


def wide(v):
    return jnp.concatenate([v, v], axis=1)


def tree_sum(terms):
    terms = list(terms)
    while len(terms) > 1:
        pairs = [terms[i : i + 2] for i in range(0, len(terms), 2)]
        terms = [p[0] + p[1] if len(p) == 2 else p[0] for p in pairs]
    return terms[0]


def small_ldl(e):
    m = [[None] * SUB for _ in range(SUB)]
    rc = [None] * SUB
    for k in range(SUB):
        rc[k] = 1.0 / e[k][k]
        for a in range(k + 1, SUB):
            m[a][k] = e[a][k] * rc[k]
        for a in range(k + 1, SUB):
            for b in range(k + 1, a + 1):
                e[a][b] = e[a][b] - m[a][k] * e[b][k]
    inv = [[None] * SUB for _ in range(SUB)]
    for b in range(SUB):
        for a in range(b + 1, SUB):
            v = m[a][b]
            for c in range(b + 1, a):
                v = v + m[a][c] * inv[c][b]
            inv[a][b] = -v
    return inv, rc, [e[k][k] for k in range(SUB)]


def factor_tiles(tiles, b0):
    count = len(tiles)
    lane = lax.broadcasted_iota(jnp.int32, (SUB, B), 1)
    sub = lax.broadcasted_iota(jnp.int32, (SUB, B), 0)
    narrow = lax.broadcasted_iota(jnp.int32, (SUB, 128), 0)
    tiles = list(tiles)
    keep = []
    update = []
    for i in range(count):
        k0 = b0 + SUB * i
        x = tiles[i]
        e = [[None] * SUB for _ in range(SUB)]
        for a in range(SUB):
            for b in range(a + 1):
                e[a][b] = jnp.broadcast_to(x[a : a + 1, k0 + b : k0 + b + 1], (SUB, 128))
        inv, rc, d = small_ldl(e)
        cols = []
        for b in range(SUB):
            v = jnp.where(narrow == b, 1.0, 0.0)
            for a in range(b + 1, SUB):
                v = jnp.where(narrow == a, inv[a][b], v)
            cols.append(v)
        pivot = d[0]
        for a in range(1, SUB):
            pivot = jnp.where(narrow == a, d[a], pivot)
        scale = wide(lax.rsqrt(pivot))
        r = tree_sum(
            wide(cols[b]) * jnp.broadcast_to(x[b : b + 1, :], (SUB, B)) for b in range(SUB)
        )
        z = 0.0
        for b in range(SUB):
            z = jnp.where(lane == k0 + b, wide(cols[b]), z)
        in_block = (lane >= k0) & (lane < k0 + SUB)
        y = jnp.where(in_block, z, r)
        if i < count - 1:
            rows = []
            for a in range(SUB):
                v = jnp.where(narrow == a, rc[a], 0.0)
                for b in range(a):
                    v = jnp.where(narrow == b, inv[a][b] * rc[a], v)
                rows.append(v)
            g = tree_sum(
                wide(rows[a]) * jnp.broadcast_to(y[a : a + 1, :], (SUB, B)) for a in range(SUB)
            )
            for j in range(i + 1, count):
                t = tiles[j]
                tiles[j] = jnp.where(in_block, 0.0, t) - tree_sum(
                    jnp.broadcast_to(t[:, k0 + b : k0 + b + 1], (SUB, B))
                    * jnp.broadcast_to(g[b : b + 1, :], (SUB, B))
                    for b in range(SUB)
                )
        scaled = y * scale
        keep.append(jnp.where(in_block & (lane > k0 + sub), r * scale, scaled))
        later = (lane >= k0 + SUB) & (lane < b0 + SUB * count)
        update.append(jnp.where(later, 0.0, scaled))
    return keep, update


def cholesky_in_place(t_ref, beside):
    count = PANEL // SUB
    tiles = [t_ref[SUB * i : SUB * (i + 1), :] for i in range(count)]
    for b0 in range(0, B, PANEL):
        b1 = b0 + PANEL
        beside(b0 // PANEL)
        keep, update = factor_tiles(tiles, b0)
        for i in range(count):
            t_ref[b0 + SUB * i : b0 + SUB * (i + 1), :] = keep[i]
        if b1 == B:
            break
        right = jnp.concatenate(update, axis=0)
        left = right.T

        def below(lo, hi):
            lanes = lax.broadcasted_iota(jnp.int32, (hi - lo, B), 1)
            old = jnp.where((lanes >= b0) & (lanes < b1), 0.0, t_ref[lo:hi, :])
            return old - jnp.dot(
                left[lo:hi], right, precision=HIGHEST, preferred_element_type=F32
            )

        ahead = below(b1, b1 + PANEL)
        tiles = [ahead[SUB * i : SUB * (i + 1), :] for i in range(count)]
        if b1 + PANEL < B:
            t_ref[b1 + PANEL :, :] = below(b1 + PANEL, B)


def factor_block(d, t_ref, beside=lambda q: None):
    t_ref[...] = 0.5 * (d + d.T)
    cholesky_in_place(t_ref, beside)
    t = t_ref[...]
    ri = lax.broadcasted_iota(jnp.int32, (B, B), 0)
    ci = lax.broadcasted_iota(jnp.int32, (B, B), 1)
    inv = jnp.where(ci <= ri, t, 0.0)
    low = jnp.where(ci > ri, t, jnp.where(ci == ri, 1.0 / t, 0.0)).T
    return low, inv


def first_kernel(a_ref, low_ref, inv_ref, t_ref):
    low_ref[...], inv_ref[...] = factor_block(a_ref[...].astype(F32), t_ref)


def factor_first(block):
    return pl.pallas_call(
        first_kernel,
        in_specs=[VMEM],
        out_specs=[VMEM, VMEM],
        out_shape=[jax.ShapeDtypeStruct((B, B), F32)] * 2,
        scratch_shapes=[pltpu.VMEM((B, B), F32)],
        compiler_params=pltpu.CompilerParams(vmem_limit_bytes=40 << 20),
        cost_estimate=pl.CostEstimate(
            flops=10_000_000_000, bytes_accessed=1 << 20, transcendentals=0
        ),
    )(block)


def split(x):
    high = x.astype(BF16)
    return high, (x - high.astype(F32)).astype(BF16)


def rest_kernel(
    scalars,
    own_ref,
    all_ref,
    low0_ref,
    inv0_ref,
    factor_ref,
    u_ref,
    rows_ref,
    corner_ref,
    t_ref,
    mine_ref,
    mine_rest,
    parts_ref,
    pan_ref,
    p_ref,
    high_ref,
    low_part_ref,
    sum_ref,
    out_ref,
    in_sems,
    out_sems,
):
    blocks = u_ref.shape[0]
    groups = blocks // GROUP
    per_panel = blocks // (B // PANEL)
    pivots = scalars[0]
    row = scalars[1]

    def fetch(i):
        part = pl.ds(i * GROUP, GROUP)
        return pltpu.make_async_copy(all_ref.at[part], rows_ref.at[part], in_sems.at[i])

    def send(i):
        part = pl.ds(i * GROUP, GROUP)
        return pltpu.make_async_copy(out_ref.at[part], u_ref.at[part], out_sems.at[i])

    def cols(t):
        return slice(t * B, (t + 1) * B)

    def take_inverse(t, inv):
        parts_ref[t, 0], parts_ref[t, 1] = split(inv)

    def own_step(t, w, low, inv):
        solved = dot_nt(w, inv, HIGHEST)
        block = jnp.where(row > t, solved, jnp.where(row == t, low, 0.0))
        factor_ref[:, cols(t)] = jnp.where(t < pivots, block, 0.0)
        panel = solved.astype(BF16)
        mine_ref[:, cols(t)] = jnp.where(t < pivots, panel, 0.0).astype(BF16)
        return panel

    def other_step(t, j):
        high, low = parts_ref[t, 0], parts_ref[t, 1]
        if t == 0:
            a = rows_ref[j, :, cols(0)]
            x = dot_nt(a, high) + dot_nt(a, low)
        else:
            wh, wl = high_ref[j], low_part_ref[j]
            x = dot_nt(wh, high) + (dot_nt(wl, high) + dot_nt(wh, low))
        return x.astype(BF16)

    for i in range(groups):
        fetch(i).start()
    inv0 = inv0_ref[...]
    take_inverse(0, inv0)
    fetch(0).wait()

    p1 = dot_nt(rows_ref[1, :, cols(0)].astype(F32), inv0, HIGHEST).astype(BF16)
    p2 = dot_nt(rows_ref[2, :, cols(0)].astype(F32), inv0, HIGHEST).astype(BF16)
    pan_ref[0] = p1
    pan_ref[1] = p2
    d = rows_ref[1, :, cols(1)].astype(F32) - dot_nt(p1, p1)
    corner_ref[0] = rows_ref[2, :, cols(1)].astype(F32) - dot_nt(p2, p1)
    corner_ref[1] = rows_ref[2, :, cols(2)].astype(F32) - dot_nt(p2, p2)

    def beside_first(q):
        if q == 0:
            panel = own_step(0, own_ref[:, cols(0)].astype(F32), low0_ref[...], inv0)
            mine_rest[0] = own_ref[:, cols(1)].astype(F32) - dot_nt(panel, pan_ref[0])
            mine_rest[1] = own_ref[:, cols(2)].astype(F32) - dot_nt(panel, pan_ref[1])
        for j in range(q * per_panel, (q + 1) * per_panel):
            if j and j % GROUP == 0:
                fetch(j // GROUP).wait()
            p = other_step(0, j)
            p_ref[j] = p
            w = rows_ref[j, :, cols(1)].astype(F32) - dot_nt(p, pan_ref[0])
            high_ref[j], low_part_ref[j] = split(w)

    low1, inv1 = factor_block(d, t_ref, beside_first)
    take_inverse(1, inv1)

    p21 = dot_nt(corner_ref[0], inv1, HIGHEST).astype(BF16)
    pan_ref[2] = p21
    d = corner_ref[1] - dot_nt(p21, p21)

    def beside_second(q):
        if q == 0:
            panel = own_step(1, mine_rest[0], low1, inv1)
            mine_rest[1] = mine_rest[1] - dot_nt(panel, pan_ref[2])
        for j in range(q * per_panel, (q + 1) * per_panel):
            p0 = p_ref[j]
            p1 = other_step(1, j)
            w = rows_ref[j, :, cols(2)].astype(F32)
            w = w - dot_nt(p0, pan_ref[1]) - dot_nt(p1, pan_ref[2])
            high_ref[j], low_part_ref[j] = split(w)
            p1 = jnp.where(1 < pivots, p1, 0.0).astype(BF16)
            sum_ref[j] = dot_nt(mine_ref[:, cols(0)], p0) + dot_nt(mine_ref[:, cols(1)], p1)

    low2, inv2 = factor_block(d, t_ref, beside_second)
    take_inverse(2, inv2)
    own_step(2, mine_rest[1], low2, inv2)

    def last(i, carry):
        part = pl.ds(i * GROUP, GROUP)
        wh = high_ref[part].reshape(GROUP * B, B)
        wl = low_part_ref[part].reshape(GROUP * B, B)
        high, low = parts_ref[2, 0], parts_ref[2, 1]
        x = dot_nt(wh, high) + (dot_nt(wl, high) + dot_nt(wh, low))
        p2 = jnp.where(2 < pivots, x.astype(BF16), 0.0).astype(BF16)
        for k in range(GROUP):
            j = i * GROUP + k
            product = dot_nt(mine_ref[:, cols(2)], p2[k * B : (k + 1) * B])
            out_ref[j] = (sum_ref[j] + product).astype(BF16)
        send(i).start()
        return carry

    lax.fori_loop(0, groups, last, 0)
    for i in range(groups):
        send(i).wait()


def factor_and_update(scalars, own, gathered, low0, inv0):
    blocks = gathered.shape[0]
    return pl.pallas_call(
        rest_kernel,
        in_specs=[pl.BlockSpec(memory_space=pltpu.SMEM), VMEM, ANY, VMEM, VMEM],
        out_specs=[VMEM, pl.BlockSpec(memory_space=pltpu.HBM)],
        out_shape=[
            jax.ShapeDtypeStruct((B, STEPS * B), F32),
            jax.ShapeDtypeStruct((blocks, B, B), BF16),
        ],
        scratch_shapes=[
            pltpu.VMEM((blocks, B, STEPS * B), BF16),
            pltpu.VMEM((2, B, B), F32),
            pltpu.VMEM((B, B), F32),
            pltpu.VMEM((B, STEPS * B), BF16),
            pltpu.VMEM((2, B, B), F32),
            pltpu.VMEM((STEPS, 2, B, B), BF16),
            pltpu.VMEM((STEPS, B, B), BF16),
            pltpu.VMEM((blocks, B, B), BF16),
            pltpu.VMEM((blocks, B, B), BF16),
            pltpu.VMEM((blocks, B, B), BF16),
            pltpu.VMEM((blocks, B, B), F32),
            pltpu.VMEM((blocks, B, B), BF16),
            pltpu.SemaphoreType.DMA((blocks // GROUP,)),
            pltpu.SemaphoreType.DMA((blocks // GROUP,)),
        ],
        compiler_params=pltpu.CompilerParams(vmem_limit_bytes=48 << 20),
        cost_estimate=pl.CostEstimate(
            flops=30_000_000_000, bytes_accessed=10 << 20, transcendentals=0
        ),
    )(scalars, own, gathered, low0, inv0)


def relayout_kernel(x_ref, y_ref):
    for i in range(GROUP):
        y_ref[i] = x_ref[:, i * B : (i + 1) * B]


def block_columns(front):
    blocks = front.shape[1] // B
    return pl.pallas_call(
        relayout_kernel,
        grid=(blocks // GROUP,),
        in_specs=[pl.BlockSpec((B, GROUP * B), lambda j: (0, j))],
        out_specs=pl.BlockSpec((GROUP, B, B), lambda j: (j, 0, 0)),
        out_shape=jax.ShapeDtypeStruct((blocks, B, B), front.dtype),
        cost_estimate=pl.CostEstimate(flops=0, bytes_accessed=4 << 20, transcendentals=0),
    )(front)


def start_sum_kernel(slots, x_ref, anc_ref, acc_ref):
    k = pl.program_id(0)

    @pl.when(k == 0)
    def _():
        acc_ref[0:2] = anc_ref[...].astype(F32)
        acc_ref[2:4] = jnp.zeros((2, B, B), F32)

    for i in range(GROUP):
        slot = slots[k * GROUP + i]

        @pl.when(slot < 4)
        def _(i=i, slot=slot):
            acc_ref[slot] += x_ref[i].astype(F32)


def end_sum_kernel(slots, x_ref, start_ref, own_ref, send_ref, acc_ref):
    k = pl.program_id(0)

    @pl.when(k == 0)
    def _():
        acc_ref[...] = start_ref[...]

    for i in range(GROUP):
        slot = slots[k * GROUP + i]

        @pl.when(slot < 4)
        def _(i=i, slot=slot):
            acc_ref[slot] -= x_ref[i].astype(F32)

    @pl.when(k == pl.num_programs(0) - 1)
    def _():
        own_ref[...] = acc_ref[0:2]
        send_ref[...] = acc_ref[2:4]


def sum_fronts(slots, x, ancestor):
    return pl.pallas_call(
        start_sum_kernel,
        grid=(x.shape[0] // GROUP,),
        in_specs=[
            pl.BlockSpec(memory_space=pltpu.SMEM),
            pl.BlockSpec((GROUP, B, B), lambda k: (k, 0, 0)),
            pl.BlockSpec((2, B, B), lambda k: (0, 0, 0)),
        ],
        out_specs=pl.BlockSpec((4, B, B), lambda k: (0, 0, 0)),
        out_shape=jax.ShapeDtypeStruct((4, B, B), F32),
        compiler_params=pltpu.CompilerParams(vmem_limit_bytes=40 << 20),
        cost_estimate=pl.CostEstimate(
            flops=4_000_000, bytes_accessed=4 << 20, transcendentals=0
        ),
    )(slots, x, ancestor)


def sum_updates(slots, x, start):
    return pl.pallas_call(
        end_sum_kernel,
        grid=(x.shape[0] // GROUP,),
        in_specs=[
            pl.BlockSpec(memory_space=pltpu.SMEM),
            pl.BlockSpec((GROUP, B, B), lambda k: (k, 0, 0)),
            pl.BlockSpec((4, B, B), lambda k: (0, 0, 0)),
        ],
        out_specs=[pl.BlockSpec((2, B, B), lambda k: (0, 0, 0))] * 2,
        out_shape=[jax.ShapeDtypeStruct((2, B, B), F32)] * 2,
        scratch_shapes=[pltpu.VMEM((4, B, B), F32)],
        compiler_params=pltpu.CompilerParams(vmem_limit_bytes=40 << 20),
        cost_estimate=pl.CostEstimate(
            flops=4_000_000, bytes_accessed=4 << 20, transcendentals=0
        ),
    )(slots, x, start)


def broadcast_first(block, row):
    size = lax.axis_size("row")
    step = size // 2
    while step:
        pairs = [(i, i + step) for i in range(0, size, 2 * step)]
        got = lax.ppermute(block, "row", pairs)
        block = jnp.where(row % (2 * step) == step, got, block)
        step //= 2
    return block


def shards(fronts, pivots, targets, ancestor):
    row = lax.axis_index("row")
    col = lax.axis_index("col")
    cols = lax.axis_size("col")
    blocks = fronts.shape[2] // B
    half = cols // 2
    groups = [list(range(half)), list(range(half, cols))]
    front = fronts[0]

    side = col // half
    block_col = col % half
    first = side * half
    piv = lax.dynamic_slice_in_dim(pivots, first, half)
    tgt = lax.dynamic_slice_in_dim(targets, first, half, axis=0)
    col_half = lax.dynamic_index_in_dim(tgt, block_col, 1, keepdims=False) // blocks
    row_half = lax.dynamic_index_in_dim(tgt, row, 1, keepdims=False) // blocks
    keep = (block_col >= piv) & (row >= piv)
    slots = jnp.where(keep, jnp.where(col_half == side, 0, 2) + row_half, 4).astype(jnp.int32)
    scalars = jnp.stack([pivots[col], row.astype(jnp.int32)])

    own, corner = lax.optimization_barrier((front[:, : STEPS * B], front[:, :B]))
    gathered = lax.all_gather(own, "row", axis=0, tiled=False)
    corner = broadcast_first(corner, row)
    low0, inv0 = factor_first(corner)
    f = lax.all_to_all(
        block_columns(front), "col", 0, 0, axis_index_groups=groups, tiled=True
    )

    start = sum_fronts(slots, f, ancestor)
    factor, u = factor_and_update(scalars, own, gathered, low0, inv0)
    u = lax.all_to_all(u, "col", 0, 0, axis_index_groups=groups, tiled=True)
    mine, sent = sum_updates(slots, u, start)
    received = lax.ppermute(sent, "col", [(c, (c + half) % cols) for c in range(cols)])
    return factor[None], mine + received


def solution(mesh):
    in_specs = (P("col", "row", None), P(), P(), P(None, "row", "col"))
    out_specs = (P("col", "row", None), P(None, "row", "col"))
    return jax.shard_map(shards, mesh=mesh, in_specs=in_specs, out_specs=out_specs, check_vma=False)
```

```python
import jax
import jax.numpy as jnp
from jax import lax
from jax.experimental import pallas as pl
from jax.experimental.pallas import tpu as pltpu
from jax.sharding import PartitionSpec as P

STEPS = 3
B = 256
SUB = 8
PANEL = 32
GROUP = 4
VMEM = pl.BlockSpec(memory_space=pltpu.VMEM)
ANY = pl.BlockSpec(memory_space=pl.ANY)
F32 = jnp.float32
BF16 = jnp.bfloat16
HIGHEST = lax.Precision.HIGHEST


def dot_nt(a, b, precision=None):
    return lax.dot_general(
        a, b, (((1,), (1,)), ((), ())), precision=precision, preferred_element_type=F32
    )


def wide(v):
    return jnp.concatenate([v, v], axis=1)


def tree_sum(terms):
    terms = list(terms)
    while len(terms) > 1:
        pairs = [terms[i : i + 2] for i in range(0, len(terms), 2)]
        terms = [p[0] + p[1] if len(p) == 2 else p[0] for p in pairs]
    return terms[0]


def small_ldl(e):
    m = [[None] * SUB for _ in range(SUB)]
    rc = [None] * SUB
    for k in range(SUB):
        rc[k] = 1.0 / e[k][k]
        for a in range(k + 1, SUB):
            m[a][k] = e[a][k] * rc[k]
        for a in range(k + 1, SUB):
            for b in range(k + 1, a + 1):
                e[a][b] = e[a][b] - m[a][k] * e[b][k]
    inv = [[None] * SUB for _ in range(SUB)]
    for b in range(SUB):
        for a in range(b + 1, SUB):
            v = m[a][b]
            for c in range(b + 1, a):
                v = v + m[a][c] * inv[c][b]
            inv[a][b] = -v
    return inv, rc, [e[k][k] for k in range(SUB)]


def factor_tiles(tiles, b0):
    count = len(tiles)
    lane = lax.broadcasted_iota(jnp.int32, (SUB, B), 1)
    sub = lax.broadcasted_iota(jnp.int32, (SUB, B), 0)
    narrow = lax.broadcasted_iota(jnp.int32, (SUB, 128), 0)
    tiles = list(tiles)
    keep = []
    update = []
    for i in range(count):
        k0 = b0 + SUB * i
        x = tiles[i]
        e = [[None] * SUB for _ in range(SUB)]
        for a in range(SUB):
            for b in range(a + 1):
                e[a][b] = jnp.broadcast_to(x[a : a + 1, k0 + b : k0 + b + 1], (SUB, 128))
        inv, rc, d = small_ldl(e)
        cols = []
        for b in range(SUB):
            v = jnp.where(narrow == b, 1.0, 0.0)
            for a in range(b + 1, SUB):
                v = jnp.where(narrow == a, inv[a][b], v)
            cols.append(v)
        pivot = d[0]
        for a in range(1, SUB):
            pivot = jnp.where(narrow == a, d[a], pivot)
        scale = wide(lax.rsqrt(pivot))
        r = tree_sum(
            wide(cols[b]) * jnp.broadcast_to(x[b : b + 1, :], (SUB, B)) for b in range(SUB)
        )
        z = 0.0
        for b in range(SUB):
            z = jnp.where(lane == k0 + b, wide(cols[b]), z)
        in_block = (lane >= k0) & (lane < k0 + SUB)
        y = jnp.where(in_block, z, r)
        if i < count - 1:
            rows = []
            for a in range(SUB):
                v = jnp.where(narrow == a, rc[a], 0.0)
                for b in range(a):
                    v = jnp.where(narrow == b, inv[a][b] * rc[a], v)
                rows.append(v)
            g = tree_sum(
                wide(rows[a]) * jnp.broadcast_to(y[a : a + 1, :], (SUB, B)) for a in range(SUB)
            )
            for j in range(i + 1, count):
                t = tiles[j]
                tiles[j] = jnp.where(in_block, 0.0, t) - tree_sum(
                    jnp.broadcast_to(t[:, k0 + b : k0 + b + 1], (SUB, B))
                    * jnp.broadcast_to(g[b : b + 1, :], (SUB, B))
                    for b in range(SUB)
                )
        scaled = y * scale
        keep.append(jnp.where(in_block & (lane > k0 + sub), r * scale, scaled))
        later = (lane >= k0 + SUB) & (lane < b0 + SUB * count)
        update.append(jnp.where(later, 0.0, scaled))
    return keep, update


def cholesky_in_place(t_ref, beside):
    count = PANEL // SUB
    tiles = [t_ref[SUB * i : SUB * (i + 1), :] for i in range(count)]
    for b0 in range(0, B, PANEL):
        b1 = b0 + PANEL
        beside(b0 // PANEL)
        keep, update = factor_tiles(tiles, b0)
        for i in range(count):
            t_ref[b0 + SUB * i : b0 + SUB * (i + 1), :] = keep[i]
        if b1 == B:
            break
        right = jnp.concatenate(update, axis=0)
        left = right.T

        def below(lo, hi):
            lanes = lax.broadcasted_iota(jnp.int32, (hi - lo, B), 1)
            old = jnp.where((lanes >= b0) & (lanes < b1), 0.0, t_ref[lo:hi, :])
            return old - jnp.dot(
                left[lo:hi], right, precision=HIGHEST, preferred_element_type=F32
            )

        ahead = below(b1, b1 + PANEL)
        tiles = [ahead[SUB * i : SUB * (i + 1), :] for i in range(count)]
        if b1 + PANEL < B:
            t_ref[b1 + PANEL :, :] = below(b1 + PANEL, B)


def factor_block(d, t_ref, beside=lambda q: None):
    t_ref[...] = 0.5 * (d + d.T)
    cholesky_in_place(t_ref, beside)
    t = t_ref[...]
    ri = lax.broadcasted_iota(jnp.int32, (B, B), 0)
    ci = lax.broadcasted_iota(jnp.int32, (B, B), 1)
    inv = jnp.where(ci <= ri, t, 0.0)
    low = jnp.where(ci > ri, t, jnp.where(ci == ri, 1.0 / t, 0.0)).T
    return low, inv


def first_kernel(a_ref, low_ref, inv_ref, t_ref):
    low_ref[...], inv_ref[...] = factor_block(a_ref[...].astype(F32), t_ref)


def factor_first(block):
    return pl.pallas_call(
        first_kernel,
        in_specs=[VMEM],
        out_specs=[VMEM, VMEM],
        out_shape=[jax.ShapeDtypeStruct((B, B), F32)] * 2,
        scratch_shapes=[pltpu.VMEM((B, B), F32)],
        compiler_params=pltpu.CompilerParams(vmem_limit_bytes=40 << 20),
        cost_estimate=pl.CostEstimate(
            flops=10_000_000_000, bytes_accessed=1 << 20, transcendentals=0
        ),
    )(block)


def split(x):
    high = x.astype(BF16)
    return high, (x - high.astype(F32)).astype(BF16)


def rest_kernel(
    scalars,
    own_ref,
    all_ref,
    low0_ref,
    inv0_ref,
    factor_ref,
    u_ref,
    rows_ref,
    corner_ref,
    t_ref,
    mine_ref,
    mine_rest,
    parts_ref,
    pan_ref,
    p_ref,
    high_ref,
    low_part_ref,
    sum_ref,
    out_ref,
    in_sems,
    out_sems,
):
    blocks = u_ref.shape[0]
    groups = blocks // GROUP
    per_panel = blocks // (B // PANEL)
    pivots = scalars[0]
    row = scalars[1]

    def fetch(i):
        part = pl.ds(i * GROUP, GROUP)
        return pltpu.make_async_copy(all_ref.at[part], rows_ref.at[part], in_sems.at[i])

    def send(i):
        part = pl.ds(i * GROUP, GROUP)
        return pltpu.make_async_copy(out_ref.at[part], u_ref.at[part], out_sems.at[i])

    def cols(t):
        return slice(t * B, (t + 1) * B)

    def take_inverse(t, inv):
        parts_ref[t, 0], parts_ref[t, 1] = split(inv)

    def own_step(t, w, low, inv):
        solved = dot_nt(w, inv, HIGHEST)
        block = jnp.where(row > t, solved, jnp.where(row == t, low, 0.0))
        factor_ref[:, cols(t)] = jnp.where(t < pivots, block, 0.0)
        panel = solved.astype(BF16)
        mine_ref[:, cols(t)] = jnp.where(t < pivots, panel, 0.0).astype(BF16)
        return panel

    def other_step(t, j):
        high, low = parts_ref[t, 0], parts_ref[t, 1]
        if t == 0:
            a = rows_ref[j, :, cols(0)]
            x = dot_nt(a, high) + dot_nt(a, low)
        else:
            wh, wl = high_ref[j], low_part_ref[j]
            x = dot_nt(wh, high) + (dot_nt(wl, high) + dot_nt(wh, low))
        return x.astype(BF16)

    for i in range(groups):
        fetch(i).start()
    inv0 = inv0_ref[...]
    take_inverse(0, inv0)
    fetch(0).wait()

    p1 = dot_nt(rows_ref[1, :, cols(0)].astype(F32), inv0, HIGHEST).astype(BF16)
    p2 = dot_nt(rows_ref[2, :, cols(0)].astype(F32), inv0, HIGHEST).astype(BF16)
    pan_ref[0] = p1
    pan_ref[1] = p2
    d = rows_ref[1, :, cols(1)].astype(F32) - dot_nt(p1, p1)
    corner_ref[0] = rows_ref[2, :, cols(1)].astype(F32) - dot_nt(p2, p1)
    corner_ref[1] = rows_ref[2, :, cols(2)].astype(F32) - dot_nt(p2, p2)

    def beside_first(q):
        if q == 0:
            panel = own_step(0, own_ref[:, cols(0)].astype(F32), low0_ref[...], inv0)
            mine_rest[0] = own_ref[:, cols(1)].astype(F32) - dot_nt(panel, pan_ref[0])
            mine_rest[1] = own_ref[:, cols(2)].astype(F32) - dot_nt(panel, pan_ref[1])
        for j in range(q * per_panel, (q + 1) * per_panel):
            if j and j % GROUP == 0:
                fetch(j // GROUP).wait()
            p = other_step(0, j)
            p_ref[j] = p
            w = rows_ref[j, :, cols(1)].astype(F32) - dot_nt(p, pan_ref[0])
            high_ref[j], low_part_ref[j] = split(w)

    low1, inv1 = factor_block(d, t_ref, beside_first)
    take_inverse(1, inv1)

    p21 = dot_nt(corner_ref[0], inv1, HIGHEST).astype(BF16)
    pan_ref[2] = p21
    d = corner_ref[1] - dot_nt(p21, p21)

    def beside_second(q):
        if q == 0:
            panel = own_step(1, mine_rest[0], low1, inv1)
            mine_rest[1] = mine_rest[1] - dot_nt(panel, pan_ref[2])
        for j in range(q * per_panel, (q + 1) * per_panel):
            p0 = p_ref[j]
            p1 = other_step(1, j)
            w = rows_ref[j, :, cols(2)].astype(F32)
            w = w - dot_nt(p0, pan_ref[1]) - dot_nt(p1, pan_ref[2])
            high_ref[j], low_part_ref[j] = split(w)
            p1 = jnp.where(1 < pivots, p1, 0.0).astype(BF16)
            sum_ref[j] = dot_nt(mine_ref[:, cols(0)], p0) + dot_nt(mine_ref[:, cols(1)], p1)

    low2, inv2 = factor_block(d, t_ref, beside_second)
    take_inverse(2, inv2)
    own_step(2, mine_rest[1], low2, inv2)

    def last(i, carry):
        part = pl.ds(i * GROUP, GROUP)
        wh = high_ref[part].reshape(GROUP * B, B)
        wl = low_part_ref[part].reshape(GROUP * B, B)
        high, low = parts_ref[2, 0], parts_ref[2, 1]
        x = dot_nt(wh, high) + (dot_nt(wl, high) + dot_nt(wh, low))
        p2 = jnp.where(2 < pivots, x.astype(BF16), 0.0).astype(BF16)
        for k in range(GROUP):
            j = i * GROUP + k
            product = dot_nt(mine_ref[:, cols(2)], p2[k * B : (k + 1) * B])
            out_ref[j] = (sum_ref[j] + product).astype(BF16)
        send(i).start()
        return carry

    lax.fori_loop(0, groups, last, 0)
    for i in range(groups):
        send(i).wait()


def factor_and_update(scalars, own, gathered, low0, inv0):
    blocks = gathered.shape[0]
    return pl.pallas_call(
        rest_kernel,
        in_specs=[pl.BlockSpec(memory_space=pltpu.SMEM), VMEM, ANY, VMEM, VMEM],
        out_specs=[VMEM, pl.BlockSpec(memory_space=pltpu.HBM)],
        out_shape=[
            jax.ShapeDtypeStruct((B, STEPS * B), F32),
            jax.ShapeDtypeStruct((blocks, B, B), BF16),
        ],
        scratch_shapes=[
            pltpu.VMEM((blocks, B, STEPS * B), BF16),
            pltpu.VMEM((2, B, B), F32),
            pltpu.VMEM((B, B), F32),
            pltpu.VMEM((B, STEPS * B), BF16),
            pltpu.VMEM((2, B, B), F32),
            pltpu.VMEM((STEPS, 2, B, B), BF16),
            pltpu.VMEM((STEPS, B, B), BF16),
            pltpu.VMEM((blocks, B, B), BF16),
            pltpu.VMEM((blocks, B, B), BF16),
            pltpu.VMEM((blocks, B, B), BF16),
            pltpu.VMEM((blocks, B, B), F32),
            pltpu.VMEM((blocks, B, B), BF16),
            pltpu.SemaphoreType.DMA((blocks // GROUP,)),
            pltpu.SemaphoreType.DMA((blocks // GROUP,)),
        ],
        compiler_params=pltpu.CompilerParams(vmem_limit_bytes=48 << 20),
        cost_estimate=pl.CostEstimate(
            flops=30_000_000_000, bytes_accessed=10 << 20, transcendentals=0
        ),
    )(scalars, own, gathered, low0, inv0)


def relayout_kernel(x_ref, y_ref):
    for i in range(GROUP):
        y_ref[i] = x_ref[:, i * B : (i + 1) * B]


def block_columns(front):
    blocks = front.shape[1] // B
    return pl.pallas_call(
        relayout_kernel,
        grid=(blocks // GROUP,),
        in_specs=[pl.BlockSpec((B, GROUP * B), lambda j: (0, j))],
        out_specs=pl.BlockSpec((GROUP, B, B), lambda j: (j, 0, 0)),
        out_shape=jax.ShapeDtypeStruct((blocks, B, B), front.dtype),
        cost_estimate=pl.CostEstimate(flops=0, bytes_accessed=4 << 20, transcendentals=0),
    )(front)


def start_sum_kernel(slots, x_ref, anc_ref, acc_ref):
    k = pl.program_id(0)

    @pl.when(k == 0)
    def _():
        acc_ref[0:2] = anc_ref[...].astype(F32)
        acc_ref[2:4] = jnp.zeros((2, B, B), F32)

    for i in range(GROUP):
        slot = slots[k * GROUP + i]

        @pl.when(slot < 4)
        def _(i=i, slot=slot):
            acc_ref[slot] += x_ref[i].astype(F32)


def end_sum_kernel(slots, x_ref, start_ref, own_ref, up_ref, down_ref, acc_ref, block_ref, sems):
    count = x_ref.shape[0]

    def fetch(k):
        return pltpu.make_async_copy(x_ref.at[k], block_ref.at[k], sems.at[k])

    for k in range(count):
        fetch(k).start()
    acc_ref[...] = start_ref[...]
    for k in range(count):
        fetch(k).wait()
        slot = slots[k]

        @pl.when(slot < 4)
        def _(k=k, slot=slot):
            acc_ref[slot] -= block_ref[k].astype(F32)

    own_ref[...] = acc_ref[0:2]
    up_ref[...] = acc_ref[2]
    down_ref[...] = acc_ref[3]


def sum_fronts(slots, x, ancestor):
    return pl.pallas_call(
        start_sum_kernel,
        grid=(x.shape[0] // GROUP,),
        in_specs=[
            pl.BlockSpec(memory_space=pltpu.SMEM),
            pl.BlockSpec((GROUP, B, B), lambda k: (k, 0, 0)),
            pl.BlockSpec((2, B, B), lambda k: (0, 0, 0)),
        ],
        out_specs=pl.BlockSpec((4, B, B), lambda k: (0, 0, 0)),
        out_shape=jax.ShapeDtypeStruct((4, B, B), F32),
        compiler_params=pltpu.CompilerParams(vmem_limit_bytes=40 << 20),
        cost_estimate=pl.CostEstimate(
            flops=4_000_000, bytes_accessed=4 << 20, transcendentals=0
        ),
    )(slots, x, ancestor)


def sum_updates(slots, x, start):
    count = x.shape[0]
    return pl.pallas_call(
        end_sum_kernel,
        in_specs=[pl.BlockSpec(memory_space=pltpu.SMEM), ANY, VMEM],
        out_specs=[VMEM, VMEM, VMEM],
        out_shape=[
            jax.ShapeDtypeStruct((2, B, B), F32),
            jax.ShapeDtypeStruct((B, B), F32),
            jax.ShapeDtypeStruct((B, B), F32),
        ],
        scratch_shapes=[
            pltpu.VMEM((4, B, B), F32),
            pltpu.VMEM((count, B, B), BF16),
            pltpu.SemaphoreType.DMA((count,)),
        ],
        compiler_params=pltpu.CompilerParams(vmem_limit_bytes=40 << 20),
        cost_estimate=pl.CostEstimate(
            flops=4_000_000, bytes_accessed=4 << 20, transcendentals=0
        ),
    )(slots, x, start)


def broadcast_first(block, row):
    size = lax.axis_size("row")
    step = size // 2
    while step:
        pairs = [(i, i + step) for i in range(0, size, 2 * step)]
        got = lax.ppermute(block, "row", pairs)
        block = jnp.where(row % (2 * step) == step, got, block)
        step //= 2
    return block


def shards(fronts, pivots, targets, ancestor):
    row = lax.axis_index("row")
    col = lax.axis_index("col")
    cols = lax.axis_size("col")
    blocks = fronts.shape[2] // B
    half = cols // 2
    groups = [list(range(half)), list(range(half, cols))]
    front = fronts[0]

    side = col // half
    block_col = col % half
    first = side * half
    piv = lax.dynamic_slice_in_dim(pivots, first, half)
    tgt = lax.dynamic_slice_in_dim(targets, first, half, axis=0)
    col_half = lax.dynamic_index_in_dim(tgt, block_col, 1, keepdims=False) // blocks
    row_half = lax.dynamic_index_in_dim(tgt, row, 1, keepdims=False) // blocks
    keep = (block_col >= piv) & (row >= piv)
    slots = jnp.where(keep, jnp.where(col_half == side, 0, 2) + row_half, 4).astype(jnp.int32)
    scalars = jnp.stack([pivots[col], row.astype(jnp.int32)])

    own, corner = lax.optimization_barrier((front[:, : STEPS * B], front[:, :B]))
    gathered = lax.all_gather(own, "row", axis=0, tiled=False)
    corner = broadcast_first(corner, row)
    low0, inv0 = factor_first(corner)
    f = lax.all_to_all(
        block_columns(front), "col", 0, 0, axis_index_groups=groups, tiled=True
    )

    start = sum_fronts(slots, f, ancestor)
    factor, u = factor_and_update(scalars, own, gathered, low0, inv0)
    u = lax.all_to_all(u, "col", 0, 0, axis_index_groups=groups, tiled=True)
    mine, up, down = sum_updates(slots, u, start)
    step = half // 2
    for _ in range(2):
        up = lax.ppermute(up, "col", [(c, (c + step) % cols) for c in range(cols)])
        down = lax.ppermute(down, "col", [(c, (c - step) % cols) for c in range(cols)])
    return factor[None], mine + jnp.stack([up, down])


def solution(mesh):
    in_specs = (P("col", "row", None), P(), P(), P(None, "row", "col"))
    out_specs = (P("col", "row", None), P(None, "row", "col"))
    return jax.shard_map(shards, mesh=mesh, in_specs=in_specs, out_specs=out_specs, check_vma=False)
```

```python
import jax
import jax.numpy as jnp
from jax import lax
from jax.experimental import pallas as pl
from jax.experimental.pallas import tpu as pltpu
from jax.sharding import PartitionSpec as P

STEPS = 3
B = 256
SUB = 8
PANEL = 32
GROUP = 4
H = B // 2
VMEM = pl.BlockSpec(memory_space=pltpu.VMEM)
ANY = pl.BlockSpec(memory_space=pl.ANY)
F32 = jnp.float32
BF16 = jnp.bfloat16
HIGHEST = lax.Precision.HIGHEST


def dot_nt(a, b, precision=None):
    return lax.dot_general(
        a, b, (((1,), (1,)), ((), ())), precision=precision, preferred_element_type=F32
    )


def wide(v):
    return jnp.concatenate([v, v], axis=1)


def tree_sum(terms):
    terms = list(terms)
    while len(terms) > 1:
        pairs = [terms[i : i + 2] for i in range(0, len(terms), 2)]
        terms = [p[0] + p[1] if len(p) == 2 else p[0] for p in pairs]
    return terms[0]


def small_ldl(e):
    m = [[None] * SUB for _ in range(SUB)]
    rc = [None] * SUB
    for k in range(SUB):
        rc[k] = 1.0 / e[k][k]
        for a in range(k + 1, SUB):
            m[a][k] = e[a][k] * rc[k]
        for a in range(k + 1, SUB):
            for b in range(k + 1, a + 1):
                e[a][b] = e[a][b] - m[a][k] * e[b][k]
    inv = [[None] * SUB for _ in range(SUB)]
    for b in range(SUB):
        for a in range(b + 1, SUB):
            v = m[a][b]
            for c in range(b + 1, a):
                v = v + m[a][c] * inv[c][b]
            inv[a][b] = -v
    return inv, rc, [e[k][k] for k in range(SUB)]


def factor_tiles(tiles, b0):
    count = len(tiles)
    lane = lax.broadcasted_iota(jnp.int32, (SUB, B), 1)
    sub = lax.broadcasted_iota(jnp.int32, (SUB, B), 0)
    narrow = lax.broadcasted_iota(jnp.int32, (SUB, 128), 0)
    tiles = list(tiles)
    keep = []
    update = []
    for i in range(count):
        k0 = b0 + SUB * i
        x = tiles[i]
        e = [[None] * SUB for _ in range(SUB)]
        for a in range(SUB):
            for b in range(a + 1):
                e[a][b] = jnp.broadcast_to(x[a : a + 1, k0 + b : k0 + b + 1], (SUB, 128))
        inv, rc, d = small_ldl(e)
        cols = []
        for b in range(SUB):
            v = jnp.where(narrow == b, 1.0, 0.0)
            for a in range(b + 1, SUB):
                v = jnp.where(narrow == a, inv[a][b], v)
            cols.append(v)
        pivot = d[0]
        for a in range(1, SUB):
            pivot = jnp.where(narrow == a, d[a], pivot)
        scale = wide(lax.rsqrt(pivot))
        r = tree_sum(
            wide(cols[b]) * jnp.broadcast_to(x[b : b + 1, :], (SUB, B)) for b in range(SUB)
        )
        z = 0.0
        for b in range(SUB):
            z = jnp.where(lane == k0 + b, wide(cols[b]), z)
        in_block = (lane >= k0) & (lane < k0 + SUB)
        y = jnp.where(in_block, z, r)
        if i < count - 1:
            rows = []
            for a in range(SUB):
                v = jnp.where(narrow == a, rc[a], 0.0)
                for b in range(a):
                    v = jnp.where(narrow == b, inv[a][b] * rc[a], v)
                rows.append(v)
            g = tree_sum(
                wide(rows[a]) * jnp.broadcast_to(y[a : a + 1, :], (SUB, B)) for a in range(SUB)
            )
            for j in range(i + 1, count):
                t = tiles[j]
                tiles[j] = jnp.where(in_block, 0.0, t) - tree_sum(
                    jnp.broadcast_to(t[:, k0 + b : k0 + b + 1], (SUB, B))
                    * jnp.broadcast_to(g[b : b + 1, :], (SUB, B))
                    for b in range(SUB)
                )
        scaled = y * scale
        keep.append(jnp.where(in_block & (lane > k0 + sub), r * scale, scaled))
        later = (lane >= k0 + SUB) & (lane < b0 + SUB * count)
        update.append(jnp.where(later, 0.0, scaled))
    return keep, update


def cholesky_in_place(t_ref, beside):
    count = PANEL // SUB
    tiles = [t_ref[SUB * i : SUB * (i + 1), :] for i in range(count)]
    for b0 in range(0, B, PANEL):
        b1 = b0 + PANEL
        beside(b0 // PANEL)
        keep, update = factor_tiles(tiles, b0)
        for i in range(count):
            t_ref[b0 + SUB * i : b0 + SUB * (i + 1), :] = keep[i]
        if b1 == B:
            break
        right = jnp.concatenate(update, axis=0)
        left = right.T

        def below(lo, hi):
            lanes = lax.broadcasted_iota(jnp.int32, (hi - lo, B), 1)
            old = jnp.where((lanes >= b0) & (lanes < b1), 0.0, t_ref[lo:hi, :])
            return old - jnp.dot(
                left[lo:hi], right, precision=HIGHEST, preferred_element_type=F32
            )

        ahead = below(b1, b1 + PANEL)
        tiles = [ahead[SUB * i : SUB * (i + 1), :] for i in range(count)]
        if b1 + PANEL < B:
            t_ref[b1 + PANEL :, :] = below(b1 + PANEL, B)


def factor_block(d, t_ref, beside=lambda q: None):
    t_ref[...] = 0.5 * (d + d.T)
    cholesky_in_place(t_ref, beside)
    t = t_ref[...]
    ri = lax.broadcasted_iota(jnp.int32, (B, B), 0)
    ci = lax.broadcasted_iota(jnp.int32, (B, B), 1)
    inv = jnp.where(ci <= ri, t, 0.0)
    low = jnp.where(ci > ri, t, jnp.where(ci == ri, 1.0 / t, 0.0)).T
    return low, inv


def first_kernel(a_ref, low_ref, inv_ref, t_ref):
    low_ref[...], inv_ref[...] = factor_block(a_ref[...].astype(F32), t_ref)


def factor_first(block):
    return pl.pallas_call(
        first_kernel,
        in_specs=[VMEM],
        out_specs=[VMEM, VMEM],
        out_shape=[jax.ShapeDtypeStruct((B, B), F32)] * 2,
        scratch_shapes=[pltpu.VMEM((B, B), F32)],
        compiler_params=pltpu.CompilerParams(vmem_limit_bytes=40 << 20),
        cost_estimate=pl.CostEstimate(
            flops=10_000_000_000, bytes_accessed=1 << 20, transcendentals=0
        ),
    )(block)


def split(x):
    high = x.astype(BF16)
    return high, (x - high.astype(F32)).astype(BF16)


def rest_kernel(
    scalars,
    own_ref,
    all_ref,
    low0_ref,
    inv0_ref,
    factor_ref,
    u_ref,
    rows_ref,
    corner_ref,
    t_ref,
    mine_ref,
    mine_rest,
    parts_ref,
    pan_ref,
    p_ref,
    high_ref,
    low_part_ref,
    sum_ref,
    out_ref,
    in_sems,
    out_sems,
):
    blocks = u_ref.shape[0]
    groups = blocks // GROUP
    per_panel = blocks // (B // PANEL)
    pivots = scalars[0]
    row = scalars[1]

    def fetch(i):
        part = pl.ds(i * GROUP, GROUP)
        return pltpu.make_async_copy(all_ref.at[part], rows_ref.at[part], in_sems.at[i])

    def send(i):
        part = pl.ds(i * GROUP, GROUP)
        return pltpu.make_async_copy(out_ref.at[part], u_ref.at[part], out_sems.at[i])

    def cols(t):
        return slice(t * B, (t + 1) * B)

    def take_inverse(t, inv):
        parts_ref[t, 0], parts_ref[t, 1] = split(inv)

    def own_step(t, w, low, inv):
        solved = dot_nt(w, inv, HIGHEST)
        block = jnp.where(row > t, solved, jnp.where(row == t, low, 0.0))
        factor_ref[:, cols(t)] = jnp.where(t < pivots, block, 0.0)
        panel = solved.astype(BF16)
        mine_ref[:, cols(t)] = jnp.where(t < pivots, panel, 0.0).astype(BF16)
        return panel

    def other_step(t, j):
        high, low = parts_ref[t, 0], parts_ref[t, 1]
        if t == 0:
            a = rows_ref[j, :, cols(0)]
            x = dot_nt(a, high) + dot_nt(a, low)
        else:
            wh, wl = high_ref[j], low_part_ref[j]
            x = dot_nt(wh, high) + (dot_nt(wl, high) + dot_nt(wh, low))
        return x.astype(BF16)

    for i in range(groups):
        fetch(i).start()
    inv0 = inv0_ref[...]
    take_inverse(0, inv0)
    fetch(0).wait()

    p1 = dot_nt(rows_ref[1, :, cols(0)].astype(F32), inv0, HIGHEST).astype(BF16)
    p2 = dot_nt(rows_ref[2, :, cols(0)].astype(F32), inv0, HIGHEST).astype(BF16)
    pan_ref[0] = p1
    pan_ref[1] = p2
    d = rows_ref[1, :, cols(1)].astype(F32) - dot_nt(p1, p1)
    corner_ref[0] = rows_ref[2, :, cols(1)].astype(F32) - dot_nt(p2, p1)
    corner_ref[1] = rows_ref[2, :, cols(2)].astype(F32) - dot_nt(p2, p2)

    def beside_first(q):
        if q == 0:
            panel = own_step(0, own_ref[:, cols(0)].astype(F32), low0_ref[...], inv0)
            mine_rest[0] = own_ref[:, cols(1)].astype(F32) - dot_nt(panel, pan_ref[0])
            mine_rest[1] = own_ref[:, cols(2)].astype(F32) - dot_nt(panel, pan_ref[1])
        for j in range(q * per_panel, (q + 1) * per_panel):
            if j and j % GROUP == 0:
                fetch(j // GROUP).wait()
            p = other_step(0, j)
            p_ref[j] = p
            w = rows_ref[j, :, cols(1)].astype(F32) - dot_nt(p, pan_ref[0])
            high_ref[j], low_part_ref[j] = split(w)

    low1, inv1 = factor_block(d, t_ref, beside_first)
    take_inverse(1, inv1)

    p21 = dot_nt(corner_ref[0], inv1, HIGHEST).astype(BF16)
    pan_ref[2] = p21
    d = corner_ref[1] - dot_nt(p21, p21)

    def beside_second(q):
        if q == 0:
            panel = own_step(1, mine_rest[0], low1, inv1)
            mine_rest[1] = mine_rest[1] - dot_nt(panel, pan_ref[2])
        for j in range(q * per_panel, (q + 1) * per_panel):
            p0 = p_ref[j]
            p1 = other_step(1, j)
            w = rows_ref[j, :, cols(2)].astype(F32)
            w = w - dot_nt(p0, pan_ref[1]) - dot_nt(p1, pan_ref[2])
            high_ref[j], low_part_ref[j] = split(w)
            p1 = jnp.where(1 < pivots, p1, 0.0).astype(BF16)
            sum_ref[j] = dot_nt(mine_ref[:, cols(0)], p0) + dot_nt(mine_ref[:, cols(1)], p1)

    low2, inv2 = factor_block(d, t_ref, beside_second)
    take_inverse(2, inv2)
    own_step(2, mine_rest[1], low2, inv2)

    def last(i, carry):
        part = pl.ds(i * GROUP, GROUP)
        wh = high_ref[part].reshape(GROUP * B, B)
        wl = low_part_ref[part].reshape(GROUP * B, B)
        high, low = parts_ref[2, 0], parts_ref[2, 1]
        x = dot_nt(wh, high) + (dot_nt(wl, high) + dot_nt(wh, low))
        p2 = jnp.where(2 < pivots, x.astype(BF16), 0.0).astype(BF16)
        for k in range(GROUP):
            j = i * GROUP + k
            product = dot_nt(mine_ref[:, cols(2)], p2[k * B : (k + 1) * B])
            out_ref[j] = (sum_ref[j] + product).astype(BF16)
        send(i).start()
        return carry

    lax.fori_loop(0, groups, last, 0)
    for i in range(groups):
        send(i).wait()


def factor_and_update(scalars, own, gathered, low0, inv0):
    blocks = gathered.shape[0]
    return pl.pallas_call(
        rest_kernel,
        in_specs=[pl.BlockSpec(memory_space=pltpu.SMEM), VMEM, ANY, VMEM, VMEM],
        out_specs=[VMEM, pl.BlockSpec(memory_space=pltpu.HBM)],
        out_shape=[
            jax.ShapeDtypeStruct((B, STEPS * B), F32),
            jax.ShapeDtypeStruct((blocks, B, B), BF16),
        ],
        scratch_shapes=[
            pltpu.VMEM((blocks, B, STEPS * B), BF16),
            pltpu.VMEM((2, B, B), F32),
            pltpu.VMEM((B, B), F32),
            pltpu.VMEM((B, STEPS * B), BF16),
            pltpu.VMEM((2, B, B), F32),
            pltpu.VMEM((STEPS, 2, B, B), BF16),
            pltpu.VMEM((STEPS, B, B), BF16),
            pltpu.VMEM((blocks, B, B), BF16),
            pltpu.VMEM((blocks, B, B), BF16),
            pltpu.VMEM((blocks, B, B), BF16),
            pltpu.VMEM((blocks, B, B), F32),
            pltpu.VMEM((blocks, B, B), BF16),
            pltpu.SemaphoreType.DMA((blocks // GROUP,)),
            pltpu.SemaphoreType.DMA((blocks // GROUP,)),
        ],
        compiler_params=pltpu.CompilerParams(vmem_limit_bytes=62 << 20),
        cost_estimate=pl.CostEstimate(
            flops=30_000_000_000, bytes_accessed=10 << 20, transcendentals=0
        ),
    )(scalars, own, gathered, low0, inv0)


def relayout_kernel(x_ref, y_ref):
    for i in range(GROUP):
        y_ref[i] = x_ref[:, i * B : (i + 1) * B]


def block_columns(front):
    blocks = front.shape[1] // B
    return pl.pallas_call(
        relayout_kernel,
        grid=(blocks // GROUP,),
        in_specs=[pl.BlockSpec((B, GROUP * B), lambda j: (0, j))],
        out_specs=pl.BlockSpec((GROUP, B, B), lambda j: (j, 0, 0)),
        out_shape=jax.ShapeDtypeStruct((blocks, B, B), front.dtype),
        cost_estimate=pl.CostEstimate(flops=0, bytes_accessed=4 << 20, transcendentals=0),
    )(front)


def start_sum_kernel(slots, x_ref, anc_ref, acc_ref):
    k = pl.program_id(0)

    @pl.when(k == 0)
    def _():
        acc_ref[0:2] = anc_ref[...].astype(F32)
        acc_ref[2:4] = jnp.zeros((2, B, B), F32)

    for i in range(GROUP):
        slot = slots[k * GROUP + i]

        @pl.when(slot < 4)
        def _(i=i, slot=slot):
            acc_ref[slot] += x_ref[i].astype(F32)


def end_sum_kernel(slots, x_ref, start_ref, own_ref, send_ref, acc_ref):
    k = pl.program_id(0)

    @pl.when(k == 0)
    def _():
        acc_ref[...] = start_ref[...]

    for i in range(GROUP):
        slot = slots[k * GROUP + i]

        @pl.when(slot < 4)
        def _(i=i, slot=slot):
            acc_ref[slot] -= x_ref[i].astype(F32)

    @pl.when(k == pl.num_programs(0) - 1)
    def _():
        own_ref[...] = acc_ref[0:2]
        send_ref[...] = acc_ref[2:4]


def sum_fronts(slots, x, ancestor):
    return pl.pallas_call(
        start_sum_kernel,
        grid=(x.shape[0] // GROUP,),
        in_specs=[
            pl.BlockSpec(memory_space=pltpu.SMEM),
            pl.BlockSpec((GROUP, B, B), lambda k: (k, 0, 0)),
            pl.BlockSpec((2, B, B), lambda k: (0, 0, 0)),
        ],
        out_specs=pl.BlockSpec((4, B, B), lambda k: (0, 0, 0)),
        out_shape=jax.ShapeDtypeStruct((4, B, B), F32),
        compiler_params=pltpu.CompilerParams(vmem_limit_bytes=40 << 20),
        cost_estimate=pl.CostEstimate(
            flops=4_000_000, bytes_accessed=4 << 20, transcendentals=0
        ),
    )(slots, x, ancestor)


def sum_updates(slots, x, start, half):
    return pl.pallas_call(
        end_sum_kernel,
        grid=(x.shape[0] // GROUP,),
        in_specs=[
            pl.BlockSpec(memory_space=pltpu.SMEM),
            pl.BlockSpec((GROUP, H, B), lambda k: (k, half, 0)),
            pl.BlockSpec((4, H, B), lambda k: (0, half, 0)),
        ],
        out_specs=[pl.BlockSpec((2, H, B), lambda k: (0, 0, 0))] * 2,
        out_shape=[jax.ShapeDtypeStruct((2, H, B), F32)] * 2,
        scratch_shapes=[pltpu.VMEM((4, H, B), F32)],
        compiler_params=pltpu.CompilerParams(vmem_limit_bytes=40 << 20),
        cost_estimate=pl.CostEstimate(
            flops=4_000_000, bytes_accessed=2 << 20, transcendentals=0
        ),
    )(slots, x, start)


def broadcast_first(block, row):
    size = lax.axis_size("row")
    step = size // 2
    while step:
        pairs = [(i, i + step) for i in range(0, size, 2 * step)]
        got = lax.ppermute(block, "row", pairs)
        block = jnp.where(row % (2 * step) == step, got, block)
        step //= 2
    return block


def shards(fronts, pivots, targets, ancestor):
    row = lax.axis_index("row")
    col = lax.axis_index("col")
    cols = lax.axis_size("col")
    blocks = fronts.shape[2] // B
    half = cols // 2
    groups = [list(range(half)), list(range(half, cols))]
    front = fronts[0]

    side = col // half
    block_col = col % half
    first = side * half
    piv = lax.dynamic_slice_in_dim(pivots, first, half)
    tgt = lax.dynamic_slice_in_dim(targets, first, half, axis=0)
    col_half = lax.dynamic_index_in_dim(tgt, block_col, 1, keepdims=False) // blocks
    row_half = lax.dynamic_index_in_dim(tgt, row, 1, keepdims=False) // blocks
    keep = (block_col >= piv) & (row >= piv)
    slots = jnp.where(keep, jnp.where(col_half == side, 0, 2) + row_half, 4).astype(jnp.int32)
    scalars = jnp.stack([pivots[col], row.astype(jnp.int32)])

    own, corner = lax.optimization_barrier((front[:, : STEPS * B], front[:, :B]))
    gathered = lax.all_gather(own, "row", axis=0, tiled=False)
    corner = broadcast_first(corner, row)
    low0, inv0 = factor_first(corner)
    f = lax.all_to_all(
        block_columns(front), "col", 0, 0, axis_index_groups=groups, tiled=True
    )

    start = sum_fronts(slots, f, ancestor)
    factor, u = factor_and_update(scalars, own, gathered, low0, inv0)
    u = lax.all_to_all(u, "col", 0, 0, axis_index_groups=groups, tiled=True)
    far = [(c, (c + half) % cols) for c in range(cols)]
    top, top_sent = sum_updates(slots, u, start, 0)
    top_got = lax.ppermute(top_sent, "col", far)
    bottom, bottom_sent = sum_updates(slots, u, start, 1)
    bottom_got = lax.ppermute(bottom_sent, "col", far)
    return factor[None], jnp.concatenate([top + top_got, bottom + bottom_got], axis=1)


def solution(mesh):
    in_specs = (P("col", "row", None), P(), P(), P(None, "row", "col"))
    out_specs = (P("col", "row", None), P(None, "row", "col"))
    return jax.shard_map(shards, mesh=mesh, in_specs=in_specs, out_specs=out_specs, check_vma=False)
```
